256 devices in a mesh: view: 8 (over x, core), depth: 4 (over y), stripe: 8 (over z).
Axes of the slice: x: 4, y: 4, z: 8, core: 2. Of those that a mesh axis runs over, the one named last changes fastest.
Arguments:
- attenuation: bfloat16 [128, 1024, 1024], P(('view', 'depth'), None, 'stripe'), parts along dimension 0, may hold values from 0 to 0.125
- material: int32 [128, 1024, 1024], P(('view', 'depth'), None, 'stripe'), parts along dimension 0, may hold values from 0 to 7
- tilt: int32 [8], P('view'), parts along dimension 0, may hold values from -3 to 3
- kernel_spectra: bfloat16 [2, 2048, 8, 2048], P(None, ('depth', 'stripe')), may hold values from -24 to 24
Outputs:
- primary: float32 [8192, 1024], P(('view', 'depth'), 'stripe'), parts along dimension 0
- scatter_image: float32 [8192, 1024], P(('view', 'depth', 'stripe')), parts along dimension 0
The draws below stay inside these ranges and needn't reach their ends.
There are 8 independent parts, one for each index of `view`. The reference program is written for one: setup_inputs(seed, part) draws one part's arguments, and reference() takes and returns one part's arrays. A program takes and returns all parts, laid end to end along the dimension named above; an argument that names none is the same for every part. Nothing has to cross between parts.
All inputs are finite; a program needn't handle non-finite values.
Results may differ from the reference program's by a relative error of at most 0.024.
Values may be sent and summed in bfloat16 or wider, within the bound.
A program may use at most 128 MiB of HBM per device.

```python
import jax
import jax.numpy as jnp
from jax import lax

N = 1024
G = 8
DEP_SLAB = 4
DEPTH = 16
PAD = 2048
N_DEPTH = 4


def place_ends(values, stream_key, low, high):
    longest = values.shape.index(max(values.shape))
    spots = []
    for shift in (0, 1):
        where = [jax.random.randint(jax.random.fold_in(stream_key, axis), (), 0, length) for axis, length in enumerate(values.shape)]
        where[longest] = (where[longest] + shift) % values.shape[longest]
        spots.append(tuple(where))
    return values.at[spots[0]].set(low).at[spots[1]].set(high)


def level_of(rng, extent, split, smallest, high):
    loudness = 1.0
    for dim, parts in split:
        heights = jax.random.uniform(jax.random.fold_in(jax.random.fold_in(rng, 6), dim), (parts,), jnp.float32, smallest / len(split), high / len(split))
        loudness = loudness * jnp.repeat(jnp.exp(heights), extent[dim] // parts).reshape((-1,) + (1,) * (len(extent) - 1 - dim))
    return loudness


def scatter_about(own_key, shape, scale, limit, pieces=(), held_as=jnp.bfloat16):
    loudness = level_of(own_key, shape, pieces, -0.22, 0.18) if pieces else 1.0
    result = jax.random.normal(own_key, shape, jnp.float32) * scale * loudness
    return jnp.minimum(jnp.maximum(result, -limit), limit).astype(held_as)


def setup_inputs(seed: int = 0, part: int = 0) -> dict:
    splits = jax.random.split(jax.random.key(seed), 5)
    part_keys = jax.random.split(jax.random.fold_in(splits[4], part), 5)
    return {
        "attenuation": jnp.clip(0.125 * jax.random.uniform(part_keys[0], (DEPTH, N, N), jnp.float32) ** level_of(part_keys[0], (DEPTH, N, N), ((0, 4), (2, 8)), -0.2, 0.2), 0.0, 0.125).astype(jnp.bfloat16),
        "material": place_ends(jax.random.randint(part_keys[1], (DEPTH, N, N), 0, G), jax.random.fold_in(part_keys[1], 1), 0, G - 1).astype(jnp.int32),
        "tilt": jax.random.randint(part_keys[2], (1,), -3, 4).astype(jnp.int32),
        "kernel_spectra": scatter_about(splits[3], (2, PAD, G, PAD), 4.0, 24.0, ((1, 32),)),
    }


def reference(attenuation, material, tilt, kernel_spectra):
    planes = jnp.arange(DEPTH).astype(jnp.int32)
    offsets = tilt[0] * planes
    row_index = jnp.arange(N).astype(jnp.int32)
    source_rows = (row_index[None, :] - offsets[:, None]) % N
    density = attenuation.astype(jnp.float32)[planes[:, None], source_rows, :]
    labels = material[planes[:, None], source_rows, :]
    thickness = jnp.zeros((G, N, N), jnp.float32)
    for slab_index in range(N_DEPTH):
        lower = slab_index * DEP_SLAB
        dens_slab = density[lower:lower + DEP_SLAB]
        label_slab = labels[lower:lower + DEP_SLAB]
        for group in range(G):
            partial_sum = jnp.sum(jnp.where(label_slab == group, dens_slab, 0.0), axis=0)
            rounded = lax.optimization_barrier(partial_sum.astype(jnp.bfloat16))
            thickness = thickness.at[group].add(rounded.astype(jnp.float32))
    primary = jnp.exp(-jnp.sum(thickness, axis=0))
    source = (primary[None] * thickness).astype(jnp.bfloat16)
    line_spectra = jnp.fft.fft(source.astype(jnp.float32), n=PAD, axis=2)
    line_real = lax.optimization_barrier(jnp.real(line_spectra).astype(jnp.bfloat16)).astype(jnp.float32)
    line_imag = lax.optimization_barrier(jnp.imag(line_spectra).astype(jnp.bfloat16)).astype(jnp.float32)
    mixed_real = jnp.zeros((PAD, PAD), jnp.float32)
    mixed_imag = jnp.zeros((PAD, PAD), jnp.float32)
    for group in range(G):
        column = jnp.fft.fft(line_real[group] + 1j * line_imag[group], n=PAD, axis=0)
        spec_real = jnp.real(column)
        spec_imag = jnp.imag(column)
        kern_real = kernel_spectra[0, :, group, :].astype(jnp.float32).T
        kern_imag = kernel_spectra[1, :, group, :].astype(jnp.float32).T
        mixed_real = mixed_real + kern_real * spec_real - kern_imag * spec_imag
        mixed_imag = mixed_imag + kern_real * spec_imag + kern_imag * spec_real
    mixed_real = lax.optimization_barrier(mixed_real.astype(jnp.bfloat16)).astype(jnp.float32)
    mixed_imag = lax.optimization_barrier(mixed_imag.astype(jnp.bfloat16)).astype(jnp.float32)
    half_back = jnp.fft.ifft(mixed_real + 1j * mixed_imag, axis=0)[:N]
    back_real = lax.optimization_barrier(jnp.real(half_back).astype(jnp.bfloat16)).astype(jnp.float32)
    back_imag = lax.optimization_barrier(jnp.imag(half_back).astype(jnp.bfloat16)).astype(jnp.float32)
    scatter_image = jnp.real(jnp.fft.ifft(back_real + 1j * back_imag, axis=1))[:, :N]
    return primary, scatter_image.astype(jnp.float32)
```

```python
import math

import jax
import jax.numpy as jnp
import ml_dtypes
import numpy as np
from jax import lax
from jax.experimental import pallas as pl
from jax.experimental.pallas import tpu as pltpu
from jax.sharding import PartitionSpec as P

G = 8
N = 1024
PAD = 2 * N
V, D, S = 8, 4, 8
B = D * S
Q = N // B
HALF = 128
EDGE = 64
BF = jnp.bfloat16
F32 = jnp.float32
MESH = pl.DeviceIdType.MESH
SCALE = 1.0 / PAD


def tables():
    d = np.arange(B)[:, None]
    m = np.arange(Q)[None, :]
    q = (64 * d + np.where((d >= B // 2) & (m == 0), 32, m)).reshape(-1)
    c = np.arange(N)
    angle = 2.0 * math.pi / PAD * (q[:, None] * c[None, :] % PAD)
    re = np.cos(angle)
    im = -np.sin(angle)
    im[0] = 1.0 - 2.0 * (c % 2)
    last = np.stack([re.reshape(B, Q, N), im.reshape(B, Q, N)], axis=1).reshape(2 * N, N)
    first = last.T.reshape(N, 8, 256).transpose(1, 0, 2)
    r = np.arange(N // 2)
    p = np.arange(N)
    cols = []
    for h in (0, 1):
        angle = 2.0 * math.pi / PAD * ((2 * r + h)[:, None] * p[None, :] % PAD)
        cols.append(np.concatenate([np.cos(angle), np.sin(angle)], axis=1))
    perm = np.zeros((2, Q, G, G, 2, Q))
    for x in range(2):
        for slot in range(Q):
            for g in range(G):
                perm[x, slot, g, g, x, slot] = 1.0
    perm = perm.reshape(512, 512)
    ones = np.kron(np.eye(Q), np.ones((1, G)))
    bf = ml_dtypes.bfloat16
    return tuple(np.ascontiguousarray(t).astype(bf) for t in (first, np.stack(cols), last, perm, ones))


def thickness_kernel(tilt_ref, att_ref, mat_ref, out_ref, att_ext, mat_ext, sem):
    y = lax.axis_index("depth")
    copies = [
        pltpu.make_async_copy(mat_ref, mat_ext.at[:, pl.ds(EDGE, N)], sem.at[0]),
        pltpu.make_async_copy(mat_ref.at[:, pl.ds(N - EDGE, EDGE)], mat_ext.at[:, pl.ds(0, EDGE)], sem.at[1]),
        pltpu.make_async_copy(mat_ref.at[:, pl.ds(0, EDGE)], mat_ext.at[:, pl.ds(EDGE + N, EDGE)], sem.at[2]),
    ]
    for copy in copies:
        copy.start()
    for plane in range(4):

        @pl.loop(0, N // 128)
        def _(i):
            row = pl.multiple_of(i * 128, 128)
            att_ext[plane, pl.ds(row + EDGE, 128), :] = att_ref[plane, pl.ds(row, 128), :].astype(F32)

        att_ext[plane, pl.ds(0, EDGE), :] = att_ref[plane, pl.ds(N - EDGE, EDGE), :].astype(F32)
        att_ext[plane, pl.ds(EDGE + N, EDGE), :] = att_ref[plane, pl.ds(0, EDGE), :].astype(F32)
    for copy in copies:
        copy.wait()
    shear = tilt_ref[0]

    for h in range(2):

        @pl.loop(0, 16)
        def _(it):
            j = it // 4
            row = pl.multiple_of((it % 4) * 32, 32)
            start = EDGE + 256 * j + 64 * (it % 4) + h
            dens = []
            kind = []
            for plane in range(4):
                at = start - shear * (4 * y + plane)
                dens.append(att_ext[plane, pl.ds(at, 32, stride=2), :])
                kind.append(mat_ext[plane, pl.ds(at, 32, stride=2), :])
            for g in range(G):
                acc = jnp.where(kind[0] == g, dens[0], 0.0)
                for plane in range(1, 4):
                    acc = acc + jnp.where(kind[plane] == g, dens[plane], 0.0)
                out_ref[h, j, g, pl.ds(row, 32), :] = acc.astype(BF)


def thickness_parts(tilt, attenuation, material):
    return pl.pallas_call(
        thickness_kernel,
        out_shape=jax.ShapeDtypeStruct((2, D, G, HALF, 128), BF),
        in_specs=[
            pl.BlockSpec(memory_space=pltpu.SMEM),
            pl.BlockSpec(memory_space=pltpu.VMEM),
            pl.BlockSpec(memory_space=pl.ANY),
        ],
        out_specs=pl.BlockSpec(memory_space=pltpu.VMEM),
        scratch_shapes=[
            pltpu.VMEM((4, N + 2 * EDGE, 128), F32),
            pltpu.VMEM((4, N + 2 * EDGE, 128), jnp.int32),
            pltpu.SemaphoreType.DMA((3,)),
        ],
        compiler_params=pltpu.CompilerParams(vmem_limit_bytes=32 * 2**20),
        name="thickness",
    )(tilt, attenuation, material)


def main_kernel(
    part,
    k_hbm,
    first_hbm,
    cols_hbm,
    last_hbm,
    perm,
    ones,
    prim_ref,
    scat_ref,
    first,
    cols,
    last,
    kown,
    krec,
    relay,
    partial,
    from_dn,
    from_up,
    source,
    strips,
    lines,
    lrec,
    spec,
    prod,
    back,
    brec,
    woven,
    load_sem,
    rs_send,
    rs_recv,
    st_send,
    st_recv,
    li_send,
    li_recv,
    ba_send,
    ba_recv,
    k_send,
    k_recv,
):
    v = lax.axis_index("view")
    y = lax.axis_index("depth")
    z = lax.axis_index("stripe")
    me = y * S + z
    high = me // 16
    up = lax.rem(y + 1, D)
    dn = lax.rem(y + 3, D)
    op = lax.rem(y + 2, D)
    sibling = v + 1 - 2 * lax.rem(v, 2)

    loads = [
        pltpu.make_async_copy(first_hbm, first, load_sem.at[0]),
        pltpu.make_async_copy(cols_hbm, cols, load_sem.at[1]),
        pltpu.make_async_copy(k_hbm.at[:, pl.ds(1, Q - 1)], kown.at[:, pl.ds(1, Q - 1)], load_sem.at[2]),
        pltpu.make_async_copy(k_hbm.at[:, pl.ds(32 * high, 1)], kown.at[:, pl.ds(0, 1)], load_sem.at[3]),
        pltpu.make_async_copy(last_hbm, last, load_sem.at[4]),
    ]

    barrier = pltpu.get_barrier_semaphore()

    @pl.loop(1, B)
    def _(k):
        to = lax.rem(me + k, B)
        pl.semaphore_signal(barrier, inc=1, device_id=(v, to // S, lax.rem(to, S)), device_id_type=MESH)

    for k in range(1, 4):
        pl.semaphore_signal(barrier, inc=1, device_id=(lax.rem(v + 2 * k, V), y, z), device_id_type=MESH)
    pl.semaphore_signal(barrier, inc=1, device_id=(sibling, y, z), device_id_type=MESH)
    pl.semaphore_wait(barrier, B - 1 + 4)

    def remote(src, dst, send, recv, to):
        return pltpu.make_async_remote_copy(
            src_ref=src, dst_ref=dst, send_sem=send, recv_sem=recv, device_id=to, device_id_type=MESH
        )

    lo, hi = pl.ds(0, 4), pl.ds(4, 4)
    to_up, to_dn = (v, up, z), (v, dn, z)

    def rs_copies(h):
        return [
            remote(part.at[h, op, lo], relay.at[h, 0], rs_send.at[h, 0], rs_recv.at[h, 0], to_up),
            remote(part.at[h, op, hi], relay.at[h, 1], rs_send.at[h, 1], rs_recv.at[h, 1], to_dn),
            remote(part.at[h, up, hi], from_dn.at[h, hi], rs_send.at[h, 2], rs_recv.at[h, 2], to_up),
            remote(part.at[h, dn, lo], from_up.at[h, lo], rs_send.at[h, 3], rs_recv.at[h, 3], to_dn),
            remote(partial.at[h, 0], from_dn.at[h, lo], rs_send.at[h, 4], rs_recv.at[h, 4], to_up),
            remote(partial.at[h, 1], from_up.at[h, hi], rs_send.at[h, 5], rs_recv.at[h, 5], to_dn),
        ]

    rs = [rs_copies(0), rs_copies(1)]
    for h in range(2):
        for i in range(4):
            rs[h][i].start()

    mirror = B - 1 - me
    zero_view = (7 - v) // 7
    k1 = []
    for i in range(4):
        m = 4 * v + i
        odd = zero_view * high if i == 0 else 0
        pos = (32 + lax.rem(32 - m, 32)) * (1 - odd)
        to = mirror * (1 - odd) + lax.rem(64 - me, 16) * odd
        k1.append(
            remote(
                k_hbm.at[:, pos], krec.at[m], k_send.at[i], k_recv.at[i], (v, to // S, lax.rem(to, S))
            )
        )
    for copy in k1:
        copy.start()
    for copy in loads:
        copy.start()

    def rs_add(h):
        for way, group in ((0, lo), (1, hi)):
            rs[h][way].wait_recv()
            block = up if way == 0 else dn

            for g in range(4):
                mine = part[h, block, 4 * way + g].astype(F32)
                partial[h, way, g] = (mine + relay[h, way, g].astype(F32)).astype(BF)
            rs[h][4 + way].start()

    def strip_copy(h, to):
        return remote(source.at[h, to], strips.at[h, z], st_send.at[h, to], st_recv.at[h, z], (v, y, to))

    def make_source(h):
        for i in range(2, 6):
            rs[h][i].wait_recv()

        @pl.loop(0, S)
        def _(k):
            to = lax.rem(z + 1 + k, S)
            row = pl.multiple_of(to * 16, 16)
            rows = pl.ds(row, 16)
            thick = []
            for g in range(G):
                thick.append(
                    part[h, y, g, rows, :].astype(F32)
                    + from_dn[h, g, rows, :].astype(F32)
                    + from_up[h, g, rows, :].astype(F32)
                )
            total = thick[0]
            for g in range(1, G):
                total = total + thick[g]
            prim = jnp.exp(-total)
            prim_ref[pl.ds(2 * row + h, 16, stride=2), :] = prim
            for g in range(G):
                source[h, to, pl.ds(16 * g, 16), :] = (prim * thick[g]).astype(BF)

            @pl.when(k < S - 1)
            def _():
                strip_copy(h, to).start()

        strips[h, z] = source[h, z]

    lane = lax.broadcasted_iota(jnp.int32, (16, 128), 1)
    left = lane < 64

    def line_copy(h, to):
        return remote(lines.at[h, to], lrec.at[h, me], li_send.at[h, to], li_recv.at[h, me], (v, to // S, lax.rem(to, S)))

    def line_local(h):
        return pltpu.make_async_copy(lines.at[h, me], lrec.at[h, me], li_recv.at[h, me])

    def make_lines(h):
        @pl.loop(1, S)
        def _(k):
            at = lax.rem(z + k, S)
            remote(source.at[h, at], strips.at[h, at], st_send.at[h, at], st_recv.at[h, at], (v, y, at)).wait_recv()

        @pl.loop(0, 8)
        def _(k):
            t = lax.rem(me // 4 + k, 8)
            lhs = jnp.concatenate([strips[h, s] for s in range(S)], axis=1)
            out = jnp.dot(lhs, first[t], preferred_element_type=F32)
            for pair in range(2):
                tile = out[:, 128 * pair : 128 * pair + 128]
                for gp in range(4):
                    even = tile[32 * gp : 32 * gp + 16]
                    odd = tile[32 * gp + 16 : 32 * gp + 32]
                    even_moved = pltpu.roll(even, 64, 1)
                    odd_moved = pltpu.roll(odd, 64, 1)
                    lines[h, 4 * t + 2 * pair, gp] = jnp.where(left, even, odd_moved).astype(BF)
                    lines[h, 4 * t + 2 * pair + 1, gp] = jnp.where(left, even_moved, odd).astype(BF)
            for i in range(4):
                to = 4 * t + i

                @pl.when(to != me)
                def _():
                    line_copy(h, to).start()

                @pl.when(to == me)
                def _():
                    line_local(h).start()

    def column_transform(h):
        line_local(h).wait()

        @pl.loop(1, B)
        def _(k):
            at = lax.rem(me + k, B)
            remote(
                lines.at[h, at], lrec.at[h, at], li_send.at[h, at], li_recv.at[h, at], (v, at // S, lax.rem(at, S))
            ).wait_recv()

        arrived = jnp.concatenate([lrec[h, :, gp].reshape(512, 128) for gp in range(4)], axis=1)
        lhs = lax.dot_general(perm[...], arrived, (((1,), (1,)), ((), ())), preferred_element_type=F32).astype(BF)

        @pl.loop(0, 8)
        def _(t):
            lanes = pl.ds(pl.multiple_of(t * 256, 256), 256)
            spec[h, :, lanes] = jnp.dot(lhs, cols[h, :, lanes], preferred_element_type=F32)

    def gather_kernel_x():
        for copy in k1:
            copy.wait_recv()
        mine = pl.ds(4 * v, 4)
        for k in range(1, 4):
            remote(
                krec.at[mine], krec.at[mine], k_send.at[3 + k], k_recv.at[3 + k], (lax.rem(v + 2 * k, V), y, z)
            ).start()
        remote(krec.at[mine], krec.at[mine], k_send.at[8], k_recv.at[8], (sibling, y, z)).start()

    def k2_arrival(k):
        at = pl.ds(4 * lax.rem(v - 2 * k + V, V), 4)
        return remote(
            krec.at[at], krec.at[at], k_send.at[3 + k], k_recv.at[3 + k], (lax.rem(v + 2 * k, V), y, z)
        )

    def gather_kernel_core():
        for k in range(1, 4):
            k2_arrival(k).wait_recv()
            at = pl.ds(4 * lax.rem(v - 2 * k + V, V), 4)
            remote(krec.at[at], krec.at[at], k_send.at[8 + k], k_recv.at[8 + k], (sibling, y, z)).start()

    def k3_arrival(k):
        at = pl.ds(4 * lax.rem(sibling - 2 * k + V, V), 4)
        return remote(krec.at[at], krec.at[at], k_send.at[8 + k], k_recv.at[8 + k], (sibling, y, z))

    rs_add(0)
    rs_add(1)
    make_source(0)
    loads[0].wait()
    gather_kernel_x()
    make_lines(0)
    make_source(1)
    gather_kernel_core()
    make_lines(1)
    loads[1].wait()
    column_transform(0)
    for k in range(4):
        k3_arrival(k).wait_recv()
    loads[2].wait()
    loads[3].wait()
    column_transform(1)

    def mix(mp, special):
        rows = 16 * mp if special else pl.multiple_of(mp * 16, 16)
        slots = pl.ds(2 * mp, 2)

        def kernel_tile(ref_slice):
            return ref_slice.astype(F32).reshape(16, 128)

        if special:
            row = lax.broadcasted_iota(jnp.int32, (16, 128), 0)
            chosen = row + 8 * me < 8
        for u in range(8):
            lanes = pl.ds(128 * u, 128)
            sins = pl.ds(N + 128 * u, 128)
            re = pl.ds(rows, 16)
            im = pl.ds(256 + rows, 16)
            vals = []
            for where, at in ((re, lanes), (im, lanes), (re, sins), (im, sins)):
                e = spec[0, where, at]
                o = spec[1, where, at]
                vals.append((e + o, e - o))
            for k in range(2):
                a, b, c, d = (val[k] for val in vals)
                plus_r, plus_i = a + d, b - c
                minus_r, minus_i = a - d, b + c
                if special:
                    plus_r = jnp.where(chosen, a, plus_r)
                    plus_i = jnp.where(chosen, -c, plus_i)
                    minus_r = jnp.where(chosen, b, minus_r)
                    minus_i = jnp.where(chosen, d, minus_i)
                at = pl.ds(N * k + 128 * u, 128)
                kr = kernel_tile(kown[0, slots, :, at])
                ki = kernel_tile(kown[1, slots, :, at])
                lr = kernel_tile(krec[slots, 0, :, at])
                li = kernel_tile(krec[slots, 1, :, at])
                mr = kr * plus_r - ki * plus_i
                mi = kr * plus_i + ki * plus_r
                nr = lr * minus_r + li * minus_i
                ni = li * minus_r - lr * minus_i
                x1, x2, x3, x4 = mr + nr, mi + ni, mi - ni, mr - nr
                if special:
                    x1 = jnp.where(chosen, mr, x1)
                    x2 = jnp.where(chosen, mi, x2)
                    x3 = jnp.where(chosen, nr, x3)
                    x4 = jnp.where(chosen, -ni, x4)
                for i, x in enumerate((x1, x2, x3, x4)):
                    prod[i, pl.ds(rows, 16), at] = x.astype(BF)

    mix(0, True)

    @pl.loop(1, 16)
    def _(mp):
        mix(mp, False)

    sums = []
    for i in range(4):
        full = jnp.dot(ones[...], prod[i], preferred_element_type=F32) * SCALE
        front, rear = full[:, :N], full[:, N:]
        sums.append(((front + rear).astype(BF), (front - rear).astype(BF)))
    total = None
    for h in range(2):
        u1, u2, u3, u4 = (s[h] for s in sums)
        wide = jnp.concatenate(
            [jnp.concatenate([u1, -u2], axis=1), jnp.concatenate([u3, u4], axis=1)], axis=0
        )
        none = jnp.zeros_like(wide)
        wide = jnp.concatenate([wide, none] if h == 0 else [none, wide], axis=0)
        one = lax.dot_general(cols[h], wide, (((1,), (1,)), ((), ())), preferred_element_type=F32)
        total = one if total is None else total + one
    back[...] = total.astype(BF).reshape(B, 16, 128)

    def back_copy(to):
        return remote(back.at[to], brec.at[me], ba_send.at[to], ba_recv.at[me], (v, to // S, lax.rem(to, S)))

    @pl.loop(1, B)
    def _(k):
        back_copy(lax.rem(me + k, B)).start()

    brec[me] = back[me]
    loads[4].wait()

    @pl.loop(1, B)
    def _(k):
        at = lax.rem(me + k, B)
        remote(back.at[at], brec.at[at], ba_send.at[at], ba_recv.at[at], (v, at // S, lax.rem(at, S))).wait_recv()

    even = []
    odd = []
    for dp in range(B // 2):
        b0 = brec[2 * dp].astype(F32)
        b1 = brec[2 * dp + 1].astype(F32)
        even.append(jnp.where(left, b0, pltpu.roll(b1, 64, 1)).astype(BF))
        odd.append(jnp.where(left, pltpu.roll(b0, 64, 1), b1).astype(BF))
    lhs = jnp.concatenate([jnp.concatenate(even, axis=1), jnp.concatenate(odd, axis=1)], axis=0)
    for t in range(4):
        lanes = pl.ds(256 * t, 256)
        image = jnp.dot(lhs, last[:, lanes], preferred_element_type=F32) * SCALE
        for half in range(2):
            tile = 2 * t + half
            woven[tile, pl.ds(0, 16, stride=2), :] = image[:16, 128 * half : 128 * half + 128]
            woven[tile, pl.ds(1, 16, stride=2), :] = image[16:, 128 * half : 128 * half + 128]
            scat_ref[:, pl.ds(128 * tile, 128)] = woven[tile]

    for h in range(2):
        for copy in rs[h]:
            copy.wait_send()

        @pl.loop(1, S)
        def _(k):
            strip_copy(h, lax.rem(z + k, S)).wait_send()

        @pl.loop(1, B)
        def _(k):
            line_copy(h, lax.rem(me + k, B)).wait_send()

    for copy in k1:
        copy.wait_send()
    for k in range(1, 4):
        k2_arrival(k).wait_send()
    for k in range(4):
        k3_arrival(k).wait_send()

    @pl.loop(1, B)
    def _(k):
        back_copy(lax.rem(me + k, B)).wait_send()


def shards(attenuation, material, tilt, kernel_spectra):
    part = thickness_parts(tilt, attenuation, material)
    first, cols, last, perm, ones = (jnp.asarray(t) for t in tables())
    vmem = pl.BlockSpec(memory_space=pltpu.VMEM)
    hbm = pl.BlockSpec(memory_space=pl.ANY)
    dma = pltpu.SemaphoreType.DMA
    return pl.pallas_call(
        main_kernel,
        out_shape=(
            jax.ShapeDtypeStruct((2 * HALF, 128), F32),
            jax.ShapeDtypeStruct((Q, N), F32),
        ),
        in_specs=[vmem, hbm, hbm, hbm, hbm, vmem, vmem],
        out_specs=(vmem, vmem),
        scratch_shapes=[
            pltpu.VMEM((8, N, 256), BF),
            pltpu.VMEM((2, 512, PAD), BF),
            pltpu.VMEM((PAD, N), BF),
            pltpu.VMEM((2, Q, G, PAD), BF),
            pltpu.VMEM((Q, 2, G, PAD), BF),
            pltpu.VMEM((2, 2, 4, HALF, 128), BF),
            pltpu.VMEM((2, 2, 4, HALF, 128), BF),
            pltpu.VMEM((2, G, HALF, 128), BF),
            pltpu.VMEM((2, G, HALF, 128), BF),
            pltpu.VMEM((2, S, 128, 128), BF),
            pltpu.VMEM((2, S, 128, 128), BF),
            pltpu.VMEM((2, B, 4, 16, 128), BF),
            pltpu.VMEM((2, B, 4, 16, 128), BF),
            pltpu.VMEM((2, 512, PAD), F32),
            pltpu.VMEM((4, Q * G, PAD), BF),
            pltpu.VMEM((B, 16, 128), BF),
            pltpu.VMEM((B, 16, 128), BF),
            pltpu.VMEM((8, Q, 128), F32),
            dma((5,)),
            dma((2, 6)),
            dma((2, 6)),
            dma((2, S)),
            dma((2, S)),
            dma((2, B)),
            dma((2, B)),
            dma((B,)),
            dma((B,)),
            dma((12,)),
            dma((12,)),
        ],
        compiler_params=pltpu.CompilerParams(
            collective_id=0, has_side_effects=True, vmem_limit_bytes=60 * 2**20
        ),
        name="scatter",
    )(part, kernel_spectra, first, cols, last, perm, ones)


def solution(mesh):
    return jax.shard_map(
        shards,
        mesh=mesh,
        in_specs=(
            P(("view", "depth"), None, "stripe"),
            P(("view", "depth"), None, "stripe"),
            P("view"),
            P(None, ("depth", "stripe"), None, None),
        ),
        out_specs=(P(("view", "depth"), "stripe"), P(("view", "depth", "stripe"), None)),
        check_vma=False,
    )
```

```python
import math

import jax
import jax.numpy as jnp
import ml_dtypes
import numpy as np
from jax import lax
from jax.experimental import pallas as pl
from jax.experimental.pallas import tpu as pltpu
from jax.sharding import PartitionSpec as P

G = 8
N = 1024
PAD = 2 * N
V, D, S = 8, 4, 8
B = D * S
Q = N // B
HALF = 128
EDGE = 64
BF = jnp.bfloat16
F32 = jnp.float32
MESH = pl.DeviceIdType.MESH
SCALE = 1.0 / PAD


def tables():
    d = np.arange(B)[:, None]
    m = np.arange(Q)[None, :]
    q = (64 * d + np.where((d >= B // 2) & (m == 0), 32, m)).reshape(-1)
    c = np.arange(N)
    angle = 2.0 * math.pi / PAD * (q[:, None] * c[None, :] % PAD)
    re = np.cos(angle)
    im = -np.sin(angle)
    im[0] = 1.0 - 2.0 * (c % 2)
    last = np.stack([re.reshape(B, Q, N), im.reshape(B, Q, N)], axis=1).reshape(2 * N, N)
    first = last.T.reshape(N, 8, 256).transpose(1, 0, 2)
    r = np.arange(N // 2)
    p = np.arange(N)
    cols = []
    for h in (0, 1):
        angle = 2.0 * math.pi / PAD * ((2 * r + h)[:, None] * p[None, :] % PAD)
        cols.append(np.concatenate([np.cos(angle), np.sin(angle)], axis=1))
    perm = np.zeros((2, Q, G, G, 2, Q))
    for x in range(2):
        for slot in range(Q):
            for g in range(G):
                perm[x, slot, g, g, x, slot] = 1.0
    perm = perm.reshape(512, 512)
    ones = np.kron(np.eye(Q), np.ones((1, G)))
    bf = ml_dtypes.bfloat16
    return tuple(np.ascontiguousarray(t).astype(bf) for t in (first, np.stack(cols), last, perm, ones))


def main_kernel(
    tilt_ref,
    att_hbm,
    mat_hbm,
    k_hbm,
    first_hbm,
    cols_hbm,
    last_hbm,
    perm,
    ones,
    prim_ref,
    scat_ref,
    att,
    att_ext,
    mat_ext,
    part,
    first,
    cols,
    last,
    kown,
    krec,
    kmid,
    relay,
    partial,
    from_dn,
    from_up,
    source,
    strips,
    lines,
    lrec,
    spec,
    prod,
    back,
    brec,
    woven,
    plane_sem,
    load_sem,
    rs_send,
    rs_recv,
    st_send,
    st_recv,
    li_send,
    li_recv,
    ba_send,
    ba_recv,
    k_send,
    k_recv,
):
    v = lax.axis_index("view")
    y = lax.axis_index("depth")
    z = lax.axis_index("stripe")
    me = y * S + z
    high = me // 16
    up = lax.rem(y + 1, D)
    dn = lax.rem(y + 3, D)
    op = lax.rem(y + 2, D)
    sibling = v + 1 - 2 * lax.rem(v, 2)

    planes = [
        pltpu.make_async_copy(att_hbm, att, plane_sem.at[0]),
        pltpu.make_async_copy(mat_hbm, mat_ext.at[:, pl.ds(EDGE, N)], plane_sem.at[1]),
        pltpu.make_async_copy(mat_hbm.at[:, pl.ds(N - EDGE, EDGE)], mat_ext.at[:, pl.ds(0, EDGE)], plane_sem.at[2]),
        pltpu.make_async_copy(mat_hbm.at[:, pl.ds(0, EDGE)], mat_ext.at[:, pl.ds(EDGE + N, EDGE)], plane_sem.at[3]),
    ]
    for copy in planes:
        copy.start()
    loads = [
        pltpu.make_async_copy(first_hbm, first, load_sem.at[0]),
        pltpu.make_async_copy(cols_hbm, cols, load_sem.at[1]),
        pltpu.make_async_copy(k_hbm.at[:, pl.ds(1, Q - 1)], kown.at[:, pl.ds(1, Q - 1)], load_sem.at[2]),
        pltpu.make_async_copy(k_hbm.at[:, pl.ds(32 * high, 1)], kown.at[:, pl.ds(0, 1)], load_sem.at[3]),
        pltpu.make_async_copy(last_hbm, last, load_sem.at[4]),
    ]

    barrier = pltpu.get_barrier_semaphore()

    @pl.loop(1, B)
    def _(k):
        to = lax.rem(me + k, B)
        pl.semaphore_signal(barrier, inc=1, device_id=(v, to // S, lax.rem(to, S)), device_id_type=MESH)

    for k in range(1, 4):
        pl.semaphore_signal(barrier, inc=1, device_id=(lax.rem(v + 2 * k, V), y, z), device_id_type=MESH)
    pl.semaphore_signal(barrier, inc=1, device_id=(sibling, y, z), device_id_type=MESH)

    planes[0].wait()
    for plane in range(4):

        @pl.loop(0, N // 128)
        def _(i):
            row = pl.multiple_of(i * 128, 128)
            att_ext[plane, pl.ds(row + EDGE, 128), :] = att[plane, pl.ds(row, 128), :].astype(F32)

        att_ext[plane, pl.ds(0, EDGE), :] = att[plane, pl.ds(N - EDGE, EDGE), :].astype(F32)
        att_ext[plane, pl.ds(EDGE + N, EDGE), :] = att[plane, pl.ds(0, EDGE), :].astype(F32)
    for copy in planes[1:]:
        copy.wait()
    for copy in loads:
        copy.start()
    shear = tilt_ref[0]

    def thicknesses(h, j):
        @pl.loop(0, 4)
        def _(c):
            start = EDGE + 256 * j + 64 * c + h
            dens = []
            kind = []
            for plane in range(4):
                at = start - shear * (4 * y + plane)
                dens.append(att_ext[plane, pl.ds(at, 32, stride=2), :])
                kind.append(mat_ext[plane, pl.ds(at, 32, stride=2), :])
            for g in range(G):
                acc = jnp.where(kind[0] == g, dens[0], 0.0)
                for plane in range(1, 4):
                    acc = acc + jnp.where(kind[plane] == g, dens[plane], 0.0)
                part[h, j, g, pl.ds(pl.multiple_of(c * 32, 32), 32), :] = acc.astype(BF)

    thicknesses(0, op)
    pl.semaphore_wait(barrier, B - 1 + 4)

    def remote(src, dst, send, recv, to):
        return pltpu.make_async_remote_copy(
            src_ref=src, dst_ref=dst, send_sem=send, recv_sem=recv, device_id=to, device_id_type=MESH
        )

    lo, hi = pl.ds(0, 4), pl.ds(4, 4)
    to_up, to_dn = (v, up, z), (v, dn, z)

    def rs_copies(h):
        return [
            remote(part.at[h, op, lo], relay.at[h, 0], rs_send.at[h, 0], rs_recv.at[h, 0], to_up),
            remote(part.at[h, op, hi], relay.at[h, 1], rs_send.at[h, 1], rs_recv.at[h, 1], to_dn),
            remote(part.at[h, up, hi], from_dn.at[h, hi], rs_send.at[h, 2], rs_recv.at[h, 2], to_up),
            remote(part.at[h, dn, lo], from_up.at[h, lo], rs_send.at[h, 3], rs_recv.at[h, 3], to_dn),
            remote(partial.at[h, 0], from_dn.at[h, lo], rs_send.at[h, 4], rs_recv.at[h, 4], to_up),
            remote(partial.at[h, 1], from_up.at[h, hi], rs_send.at[h, 5], rs_recv.at[h, 5], to_dn),
        ]

    rs = [rs_copies(0), rs_copies(1)]
    rs[0][0].start()
    rs[0][1].start()
    thicknesses(0, up)
    thicknesses(0, dn)
    rs[0][2].start()
    rs[0][3].start()

    across = (v, y, S - 1 - z)
    over = (v, D - 1 - y, z)
    k1 = []
    k2 = []
    for i in range(4):
        pos = 32 + lax.rem(32 - (4 * v + i), 32)
        k1.append(remote(k_hbm.at[:, pos], kmid.at[i], k_send.at[12 + i], k_recv.at[12 + i], across))
        k2.append(remote(kmid.at[i], krec.at[4 * v + i], k_send.at[i], k_recv.at[i], over))
    single = (B - 1 - me) * (1 - high) + lax.rem(64 - me, 16) * high
    k_single = remote(
        k_hbm.at[:, 32 * (1 - high)], krec.at[0], k_send.at[0], k_recv.at[0], (v, single // S, lax.rem(single, S))
    )
    for copy in k1[1:]:
        copy.start()

    @pl.when(v == 0)
    def _():
        k_single.start()

    @pl.when(v > 0)
    def _():
        k1[0].start()

    def turn_kernel():
        for i in range(1, 4):
            k1[i].wait_recv()
            k2[i].start()

        @pl.when(v > 0)
        def _():
            k1[0].wait_recv()
            k2[0].start()

    def rs_add(h):
        for way, group in ((0, lo), (1, hi)):
            rs[h][way].wait_recv()
            block = up if way == 0 else dn

            for g in range(4):
                mine = part[h, block, 4 * way + g].astype(F32)
                partial[h, way, g] = (mine + relay[h, way, g].astype(F32)).astype(BF)
            rs[h][4 + way].start()

    def strip_copy(h, to):
        return remote(source.at[h, to], strips.at[h, z], st_send.at[h, to], st_recv.at[h, z], (v, y, to))

    def make_source(h):
        for i in range(2, 6):
            rs[h][i].wait_recv()

        @pl.loop(0, S)
        def _(k):
            to = lax.rem(z + 1 + k, S)
            row = pl.multiple_of(to * 16, 16)
            rows = pl.ds(row, 16)
            thick = []
            for g in range(G):
                thick.append(
                    part[h, y, g, rows, :].astype(F32)
                    + from_dn[h, g, rows, :].astype(F32)
                    + from_up[h, g, rows, :].astype(F32)
                )
            total = thick[0]
            for g in range(1, G):
                total = total + thick[g]
            prim = jnp.exp(-total)
            prim_ref[pl.ds(2 * row + h, 16, stride=2), :] = prim
            for g in range(G):
                source[h, to, pl.ds(16 * g, 16), :] = (prim * thick[g]).astype(BF)

            @pl.when(k < S - 1)
            def _():
                strip_copy(h, to).start()

        strips[h, z] = source[h, z]

    lane = lax.broadcasted_iota(jnp.int32, (16, 128), 1)
    left = lane < 64

    def line_copy(h, to):
        return remote(lines.at[h, to], lrec.at[h, me], li_send.at[h, to], li_recv.at[h, me], (v, to // S, lax.rem(to, S)))

    def line_local(h):
        return pltpu.make_async_copy(lines.at[h, me], lrec.at[h, me], li_recv.at[h, me])

    def make_lines(h):
        @pl.loop(1, S)
        def _(k):
            at = lax.rem(z + k, S)
            remote(source.at[h, at], strips.at[h, at], st_send.at[h, at], st_recv.at[h, at], (v, y, at)).wait_recv()

        @pl.loop(0, 8)
        def _(k):
            t = lax.rem(me // 4 + k, 8)
            lhs = jnp.concatenate([strips[h, s] for s in range(S)], axis=1)
            out = jnp.dot(lhs, first[t], preferred_element_type=F32)
            for pair in range(2):
                tile = out[:, 128 * pair : 128 * pair + 128]
                for gp in range(4):
                    even = tile[32 * gp : 32 * gp + 16]
                    odd = tile[32 * gp + 16 : 32 * gp + 32]
                    even_moved = pltpu.roll(even, 64, 1)
                    odd_moved = pltpu.roll(odd, 64, 1)
                    lines[h, 4 * t + 2 * pair, gp] = jnp.where(left, even, odd_moved).astype(BF)
                    lines[h, 4 * t + 2 * pair + 1, gp] = jnp.where(left, even_moved, odd).astype(BF)
            for i in range(4):
                to = 4 * t + i

                @pl.when(to != me)
                def _():
                    line_copy(h, to).start()

                @pl.when(to == me)
                def _():
                    line_local(h).start()

    def column_transform(h):
        line_local(h).wait()

        @pl.loop(1, B)
        def _(k):
            at = lax.rem(me + k, B)
            remote(
                lines.at[h, at], lrec.at[h, at], li_send.at[h, at], li_recv.at[h, at], (v, at // S, lax.rem(at, S))
            ).wait_recv()

        arrived = jnp.concatenate([lrec[h, :, gp].reshape(512, 128) for gp in range(4)], axis=1)
        lhs = lax.dot_general(perm[...], arrived, (((1,), (1,)), ((), ())), preferred_element_type=F32).astype(BF)

        @pl.loop(0, 8)
        def _(t):
            lanes = pl.ds(pl.multiple_of(t * 256, 256), 256)
            spec[h, :, lanes] = jnp.dot(lhs, cols[h, :, lanes], preferred_element_type=F32)

    def gather_kernel_x():
        for copy in k2:
            copy.wait_recv()
        mine = pl.ds(4 * v, 4)
        for k in range(1, 4):
            remote(
                krec.at[mine], krec.at[mine], k_send.at[3 + k], k_recv.at[3 + k], (lax.rem(v + 2 * k, V), y, z)
            ).start()
        remote(krec.at[mine], krec.at[mine], k_send.at[8], k_recv.at[8], (sibling, y, z)).start()

    def k2_arrival(k):
        at = pl.ds(4 * lax.rem(v - 2 * k + V, V), 4)
        return remote(
            krec.at[at], krec.at[at], k_send.at[3 + k], k_recv.at[3 + k], (lax.rem(v + 2 * k, V), y, z)
        )

    def gather_kernel_core():
        for k in range(1, 4):
            k2_arrival(k).wait_recv()
            at = pl.ds(4 * lax.rem(v - 2 * k + V, V), 4)
            remote(krec.at[at], krec.at[at], k_send.at[8 + k], k_recv.at[8 + k], (sibling, y, z)).start()

    def k3_arrival(k):
        at = pl.ds(4 * lax.rem(sibling - 2 * k + V, V), 4)
        return remote(krec.at[at], krec.at[at], k_send.at[8 + k], k_recv.at[8 + k], (sibling, y, z))

    thicknesses(0, y)
    for j in (op, up, dn, y):
        thicknesses(1, j)
    rs_add(0)
    for copy in rs[0]:
        copy.wait_send()
    for copy in rs[1][:4]:
        copy.start()
    make_source(0)
    rs_add(1)
    turn_kernel()
    loads[0].wait()
    make_lines(0)
    gather_kernel_x()
    make_source(1)
    make_lines(1)
    loads[1].wait()
    column_transform(0)
    gather_kernel_core()
    column_transform(1)
    for k in range(4):
        k3_arrival(k).wait_recv()
    loads[2].wait()
    loads[3].wait()

    def mix(mp, special):
        rows = 16 * mp if special else pl.multiple_of(mp * 16, 16)
        slots = pl.ds(2 * mp, 2)

        def kernel_tile(ref_slice):
            return ref_slice.astype(F32).reshape(16, 128)

        if special:
            row = lax.broadcasted_iota(jnp.int32, (16, 128), 0)
            chosen = row + 8 * me < 8
        for u in range(8):
            lanes = pl.ds(128 * u, 128)
            sins = pl.ds(N + 128 * u, 128)
            re = pl.ds(rows, 16)
            im = pl.ds(256 + rows, 16)
            vals = []
            for where, at in ((re, lanes), (im, lanes), (re, sins), (im, sins)):
                e = spec[0, where, at]
                o = spec[1, where, at]
                vals.append((e + o, e - o))
            for k in range(2):
                a, b, c, d = (val[k] for val in vals)
                plus_r, plus_i = a + d, b - c
                minus_r, minus_i = a - d, b + c
                if special:
                    plus_r = jnp.where(chosen, a, plus_r)
                    plus_i = jnp.where(chosen, -c, plus_i)
                    minus_r = jnp.where(chosen, b, minus_r)
                    minus_i = jnp.where(chosen, d, minus_i)
                at = pl.ds(N * k + 128 * u, 128)
                kr = kernel_tile(kown[0, slots, :, at])
                ki = kernel_tile(kown[1, slots, :, at])
                lr = kernel_tile(krec[slots, 0, :, at])
                li = kernel_tile(krec[slots, 1, :, at])
                mr = kr * plus_r - ki * plus_i
                mi = kr * plus_i + ki * plus_r
                nr = lr * minus_r + li * minus_i
                ni = li * minus_r - lr * minus_i
                x1, x2, x3, x4 = mr + nr, mi + ni, mi - ni, mr - nr
                if special:
                    x1 = jnp.where(chosen, mr, x1)
                    x2 = jnp.where(chosen, mi, x2)
                    x3 = jnp.where(chosen, nr, x3)
                    x4 = jnp.where(chosen, -ni, x4)
                for i, x in enumerate((x1, x2, x3, x4)):
                    prod[i, pl.ds(rows, 16), at] = x.astype(BF)

    mix(0, True)

    @pl.loop(1, 16)
    def _(mp):
        mix(mp, False)

    sums = []
    for i in range(4):
        full = jnp.dot(ones[...], prod[i], preferred_element_type=F32) * SCALE
        front, rear = full[:, :N], full[:, N:]
        sums.append(((front + rear).astype(BF), (front - rear).astype(BF)))
    total = None
    for h in range(2):
        u1, u2, u3, u4 = (s[h] for s in sums)
        wide = jnp.concatenate(
            [jnp.concatenate([u1, -u2], axis=1), jnp.concatenate([u3, u4], axis=1)], axis=0
        )
        none = jnp.zeros_like(wide)
        wide = jnp.concatenate([wide, none] if h == 0 else [none, wide], axis=0)
        one = lax.dot_general(cols[h], wide, (((1,), (1,)), ((), ())), preferred_element_type=F32)
        total = one if total is None else total + one
    back[...] = total.astype(BF).reshape(B, 16, 128)

    def back_copy(to):
        return remote(back.at[to], brec.at[me], ba_send.at[to], ba_recv.at[me], (v, to // S, lax.rem(to, S)))

    @pl.loop(1, B)
    def _(k):
        back_copy(lax.rem(me + k, B)).start()

    brec[me] = back[me]
    loads[4].wait()

    @pl.loop(1, B)
    def _(k):
        at = lax.rem(me + k, B)
        remote(back.at[at], brec.at[at], ba_send.at[at], ba_recv.at[at], (v, at // S, lax.rem(at, S))).wait_recv()

    even = []
    odd = []
    for dp in range(B // 2):
        b0 = brec[2 * dp].astype(F32)
        b1 = brec[2 * dp + 1].astype(F32)
        even.append(jnp.where(left, b0, pltpu.roll(b1, 64, 1)).astype(BF))
        odd.append(jnp.where(left, pltpu.roll(b0, 64, 1), b1).astype(BF))
    lhs = jnp.concatenate([jnp.concatenate(even, axis=1), jnp.concatenate(odd, axis=1)], axis=0)
    for t in range(4):
        lanes = pl.ds(256 * t, 256)
        image = jnp.dot(lhs, last[:, lanes], preferred_element_type=F32) * SCALE
        for half in range(2):
            tile = 2 * t + half
            woven[tile, pl.ds(0, 16, stride=2), :] = image[:16, 128 * half : 128 * half + 128]
            woven[tile, pl.ds(1, 16, stride=2), :] = image[16:, 128 * half : 128 * half + 128]
            scat_ref[:, pl.ds(128 * tile, 128)] = woven[tile]

    for copy in rs[1]:
        copy.wait_send()
    for h in range(2):

        @pl.loop(1, S)
        def _(k):
            strip_copy(h, lax.rem(z + k, S)).wait_send()

        @pl.loop(1, B)
        def _(k):
            line_copy(h, lax.rem(me + k, B)).wait_send()

    for copy in k1[1:] + k2:
        copy.wait_send()

    @pl.when(v > 0)
    def _():
        k1[0].wait_send()

    for k in range(1, 4):
        k2_arrival(k).wait_send()
    for k in range(4):
        k3_arrival(k).wait_send()

    @pl.loop(1, B)
    def _(k):
        back_copy(lax.rem(me + k, B)).wait_send()


def finish_kernel(prim_in, scat_in, prim_out, scat_out):
    prim_out[...] = prim_in[...]
    scat_out[...] = scat_in[...]


def shards(attenuation, material, tilt, kernel_spectra):
    first, cols, last, perm, ones = (jnp.asarray(t) for t in tables())
    vmem = pl.BlockSpec(memory_space=pltpu.VMEM)
    hbm = pl.BlockSpec(memory_space=pl.ANY)
    dma = pltpu.SemaphoreType.DMA
    shapes = (jax.ShapeDtypeStruct((2 * HALF, 128), F32), jax.ShapeDtypeStruct((Q, N), F32))
    results = pl.pallas_call(
        main_kernel,
        out_shape=shapes,
        in_specs=[pl.BlockSpec(memory_space=pltpu.SMEM), hbm, hbm, hbm, hbm, hbm, hbm, vmem, vmem],
        out_specs=(vmem, vmem),
        scratch_shapes=[
            pltpu.VMEM((4, N, 128), BF),
            pltpu.VMEM((4, N + 2 * EDGE, 128), F32),
            pltpu.VMEM((4, N + 2 * EDGE, 128), jnp.int32),
            pltpu.VMEM((2, D, G, HALF, 128), BF),
            pltpu.VMEM((8, N, 256), BF),
            pltpu.VMEM((2, 512, PAD), BF),
            pltpu.VMEM((PAD, N), BF),
            pltpu.VMEM((2, Q, G, PAD), BF),
            pltpu.VMEM((Q, 2, G, PAD), BF),
            pltpu.VMEM((4, 2, G, PAD), BF),
            pltpu.VMEM((2, 2, 4, HALF, 128), BF),
            pltpu.VMEM((2, 2, 4, HALF, 128), BF),
            pltpu.VMEM((2, G, HALF, 128), BF),
            pltpu.VMEM((2, G, HALF, 128), BF),
            pltpu.VMEM((2, S, 128, 128), BF),
            pltpu.VMEM((2, S, 128, 128), BF),
            pltpu.VMEM((2, B, 4, 16, 128), BF),
            pltpu.VMEM((2, B, 4, 16, 128), BF),
            pltpu.VMEM((2, 512, PAD), F32),
            pltpu.VMEM((4, Q * G, PAD), BF),
            pltpu.VMEM((B, 16, 128), BF),
            pltpu.VMEM((B, 16, 128), BF),
            pltpu.VMEM((8, Q, 128), F32),
            dma((4,)),
            dma((5,)),
            dma((2, 6)),
            dma((2, 6)),
            dma((2, S)),
            dma((2, S)),
            dma((2, B)),
            dma((2, B)),
            dma((B,)),
            dma((B,)),
            dma((16,)),
            dma((16,)),
        ],
        compiler_params=pltpu.CompilerParams(
            collective_id=0, has_side_effects=True, vmem_limit_bytes=60 * 2**20
        ),
        name="scatter",
    )(tilt, attenuation, material, kernel_spectra, first, cols, last, perm, ones)
    return pl.pallas_call(
        finish_kernel,
        out_shape=shapes,
        in_specs=[vmem, vmem],
        out_specs=(vmem, vmem),
        name="finish",
    )(*results)


def solution(mesh):
    return jax.shard_map(
        shards,
        mesh=mesh,
        in_specs=(
            P(("view", "depth"), None, "stripe"),
            P(("view", "depth"), None, "stripe"),
            P("view"),
            P(None, ("depth", "stripe"), None, None),
        ),
        out_specs=(P(("view", "depth"), "stripe"), P(("view", "depth", "stripe"), None)),
        check_vma=False,
    )
```

```python
import math

import jax
import jax.numpy as jnp
import ml_dtypes
import numpy as np
from jax import lax
from jax.experimental import pallas as pl
from jax.experimental.pallas import tpu as pltpu
from jax.sharding import PartitionSpec as P

G = 8
N = 1024
PAD = 2 * N
V, D, S = 8, 4, 8
B = D * S
Q = N // B
H = 4
PART = 64
F = PAD // H
EDGE = 64
BF = jnp.bfloat16
F32 = jnp.float32
MESH = pl.DeviceIdType.MESH
SCALE = 1.0 / PAD


def tables():
    d = np.arange(B)[:, None]
    m = np.arange(Q)[None, :]
    q = (64 * d + np.where((d >= B // 2) & (m == 0), 32, m)).reshape(-1)
    c = np.arange(N)
    angle = 2.0 * math.pi / PAD * (q[:, None] * c[None, :] % PAD)
    re = np.cos(angle)
    im = -np.sin(angle)
    im[0] = 1.0 - 2.0 * (c % 2)
    last = np.stack([re.reshape(B, Q, N), im.reshape(B, Q, N)], axis=1).reshape(2 * N, N)
    first = last.T.reshape(N, 8, 256).transpose(1, 0, 2)
    r = np.arange(N // H)
    p = np.arange(F)
    cols = []
    for h in range(H):
        angle = 2.0 * math.pi / PAD * ((H * r + h)[:, None] * p[None, :] % PAD)
        cols.append(np.concatenate([np.cos(angle), np.sin(angle)], axis=1))
    perm = np.zeros((2, Q, G, G, 2, Q))
    for x in range(2):
        for slot in range(Q):
            for g in range(G):
                perm[x, slot, g, g, x, slot] = 1.0
    perm = perm.reshape(512, 512)
    ones = np.kron(np.eye(Q), np.ones((1, G)))
    bf = ml_dtypes.bfloat16
    return tuple(np.ascontiguousarray(t).astype(bf) for t in (first, np.stack(cols), last, perm, ones))


def main_kernel(
    tilt_ref,
    att_hbm,
    mat_hbm,
    k_hbm,
    first_hbm,
    cols_hbm,
    last_hbm,
    perm_hbm,
    ones_hbm,
    prim_ref,
    scat_ref,
    att,
    att_ext,
    mat_ext,
    part,
    first,
    cols,
    last,
    perm,
    ones,
    kown,
    krec,
    kmid,
    relay,
    partial,
    from_dn,
    from_up,
    source,
    strips,
    lines,
    lrec,
    spec,
    prod,
    back,
    brec,
    woven,
    plane_sem,
    load_sem,
    rs_send,
    rs_recv,
    st_send,
    st_recv,
    li_send,
    li_recv,
    ba_send,
    ba_recv,
    k_send,
    k_recv,
):
    v = lax.axis_index("view")
    y = lax.axis_index("depth")
    z = lax.axis_index("stripe")
    me = y * S + z
    high = me // 16
    up = lax.rem(y + 1, D)
    dn = lax.rem(y + 3, D)
    op = lax.rem(y + 2, D)
    sibling = v + 1 - 2 * lax.rem(v, 2)

    planes = [
        pltpu.make_async_copy(att_hbm, att, plane_sem.at[0]),
        pltpu.make_async_copy(mat_hbm, mat_ext.at[:, pl.ds(EDGE, N)], plane_sem.at[1]),
        pltpu.make_async_copy(mat_hbm.at[:, pl.ds(N - EDGE, EDGE)], mat_ext.at[:, pl.ds(0, EDGE)], plane_sem.at[2]),
        pltpu.make_async_copy(mat_hbm.at[:, pl.ds(0, EDGE)], mat_ext.at[:, pl.ds(EDGE + N, EDGE)], plane_sem.at[3]),
    ]
    for copy in planes:
        copy.start()
    loads = [
        pltpu.make_async_copy(first_hbm, first, load_sem.at[0]),
        pltpu.make_async_copy(cols_hbm, cols, load_sem.at[1]),
        pltpu.make_async_copy(k_hbm.at[:, pl.ds(1, Q - 1)], kown.at[:, pl.ds(1, Q - 1)], load_sem.at[2]),
        pltpu.make_async_copy(k_hbm.at[:, pl.ds(32 * high, 1)], kown.at[:, pl.ds(0, 1)], load_sem.at[3]),
        pltpu.make_async_copy(last_hbm, last, load_sem.at[4]),
        pltpu.make_async_copy(perm_hbm, perm, load_sem.at[5]),
        pltpu.make_async_copy(ones_hbm, ones, load_sem.at[6]),
    ]

    barrier = pltpu.get_barrier_semaphore()

    @pl.loop(1, B)
    def _(k):
        to = lax.rem(me + k, B)
        pl.semaphore_signal(barrier, inc=1, device_id=(v, to // S, lax.rem(to, S)), device_id_type=MESH)

    for k in range(1, 4):
        pl.semaphore_signal(barrier, inc=1, device_id=(lax.rem(v + 2 * k, V), y, z), device_id_type=MESH)
    pl.semaphore_signal(barrier, inc=1, device_id=(sibling, y, z), device_id_type=MESH)

    pl.semaphore_wait(barrier, B - 1 + 4)
    def remote(src, dst, send, recv, to):
        return pltpu.make_async_remote_copy(
            src_ref=src, dst_ref=dst, send_sem=send, recv_sem=recv, device_id=to, device_id_type=MESH
        )

    lo, hi = pl.ds(0, 4), pl.ds(4, 4)
    to_up, to_dn = (v, up, z), (v, dn, z)

    def rs_copies(h):
        return [
            remote(part.at[h, op, lo], relay.at[h, 0], rs_send.at[h, 0], rs_recv.at[h, 0], to_up),
            remote(part.at[h, op, hi], relay.at[h, 1], rs_send.at[h, 1], rs_recv.at[h, 1], to_dn),
            remote(part.at[h, up, hi], from_dn.at[h, hi], rs_send.at[h, 2], rs_recv.at[h, 2], to_up),
            remote(part.at[h, dn, lo], from_up.at[h, lo], rs_send.at[h, 3], rs_recv.at[h, 3], to_dn),
            remote(partial.at[h, 0], from_dn.at[h, lo], rs_send.at[h, 4], rs_recv.at[h, 4], to_up),
            remote(partial.at[h, 1], from_up.at[h, hi], rs_send.at[h, 5], rs_recv.at[h, 5], to_dn),
        ]

    rs = [rs_copies(h) for h in range(H)]
    across = (v, y, S - 1 - z)
    over = (v, D - 1 - y, z)
    k1 = []
    k2 = []
    for i in range(4):
        pos = 32 + lax.rem(32 - (4 * v + i), 32)
        k1.append(remote(k_hbm.at[:, pos], kmid.at[i], k_send.at[12 + i], k_recv.at[12 + i], across))
        k2.append(remote(kmid.at[i], krec.at[4 * v + i], k_send.at[i], k_recv.at[i], over))
    single = (B - 1 - me) * (1 - high) + lax.rem(64 - me, 16) * high
    k_single = remote(
        k_hbm.at[:, 32 * (1 - high)], krec.at[0], k_send.at[0], k_recv.at[0], (v, single // S, lax.rem(single, S))
    )
    def fetch_kernel():
        for copy in k1[1:]:
            copy.start()

        @pl.when(v == 0)
        def _():
            k_single.start()

        @pl.when(v > 0)
        def _():
            k1[0].start()

    fetch_kernel()
    planes[0].wait()
    for plane in range(4):

        @pl.loop(0, N // 128)
        def _(i):
            row = pl.multiple_of(i * 128, 128)
            att_ext[plane, pl.ds(row + EDGE, 128), :] = att[plane, pl.ds(row, 128), :].astype(F32)

        att_ext[plane, pl.ds(0, EDGE), :] = att[plane, pl.ds(N - EDGE, EDGE), :].astype(F32)
        att_ext[plane, pl.ds(EDGE + N, EDGE), :] = att[plane, pl.ds(0, EDGE), :].astype(F32)
    for copy in planes[1:]:
        copy.wait()
    shear = tilt_ref[0]

    def thicknesses(h, j):
        @pl.loop(0, 2)
        def _(c):
            start = EDGE + 256 * j + 128 * c + h
            dens = []
            kind = []
            for plane in range(4):
                at = start - shear * (4 * y + plane)
                dens.append(att_ext[plane, pl.ds(at, 32, stride=H), :])
                kind.append(mat_ext[plane, pl.ds(at, 32, stride=H), :])
            for g in range(G):
                acc = jnp.where(kind[0] == g, dens[0], 0.0)
                for plane in range(1, 4):
                    acc = acc + jnp.where(kind[plane] == g, dens[plane], 0.0)
                part[h, j, g, pl.ds(pl.multiple_of(c * 32, 32), 32), :] = acc.astype(BF)

    def turn_kernel():
        for i in range(1, 4):
            k1[i].wait_recv()
            k2[i].start()

        @pl.when(v > 0)
        def _():
            k1[0].wait_recv()
            k2[0].start()

    def rs_add(h):
        for way, group in ((0, lo), (1, hi)):
            rs[h][way].wait_recv()
            block = up if way == 0 else dn

            for g in range(4):
                mine = part[h, block, 4 * way + g].astype(F32)
                partial[h, way, g] = (mine + relay[h, way, g].astype(F32)).astype(BF)
            rs[h][4 + way].start()

    def strip_copy(h, to):
        return remote(source.at[h, to], strips.at[h, z], st_send.at[h, to], st_recv.at[h, z], (v, y, to))

    def make_source(h):
        for i in range(2, 6):
            rs[h][i].wait_recv()

        for k in range(S // 2):
            pair = lax.rem(z // 2 + 1 + k, S // 2)
            row = pl.multiple_of(pair * 16, 16)
            rows = pl.ds(row, 16)
            thick = []
            for g in range(G):
                thick.append(
                    part[h, y, g, rows, :].astype(F32)
                    + from_dn[h, g, rows, :].astype(F32)
                    + from_up[h, g, rows, :].astype(F32)
                )
            total = thick[0]
            for g in range(1, G):
                total = total + thick[g]
            prim = jnp.exp(-total)
            prim_ref[pl.ds(H * row + h, 16, stride=H), :] = prim
            values = [prim * thick[g] for g in range(G)]
            for side in range(2):
                to = 2 * pair + side
                cut = slice(8 * side, 8 * side + 8)
                for gp in range(G // 2):
                    both = jnp.concatenate([values[2 * gp][cut], values[2 * gp + 1][cut]], axis=0)
                    source[h, to, pl.ds(16 * gp, 16), :] = both.astype(BF)

                @pl.when(to != z)
                def _():
                    strip_copy(h, to).start()

        strips[h, z] = source[h, z]

    left = lax.broadcasted_iota(jnp.int32, (8, 128), 1) < 64
    left16 = lax.broadcasted_iota(jnp.int32, (16, 128), 1) < 64

    def line_copy(h, to):
        return remote(lines.at[h, to], lrec.at[h, me], li_send.at[h, to], li_recv.at[h, me], (v, to // S, lax.rem(to, S)))

    def line_local(h):
        return pltpu.make_async_copy(lines.at[h, me], lrec.at[h, me], li_recv.at[h, me])

    def make_lines(h):
        @pl.loop(1, S)
        def _(k):
            at = lax.rem(z + k, S)
            remote(source.at[h, at], strips.at[h, at], st_send.at[h, at], st_recv.at[h, at], (v, y, at)).wait_recv()

        @pl.loop(0, 8)
        def _(k):
            step = (k + 1) // 2
            t = lax.rem(me // 4 + 8 + step * (1 - 2 * lax.rem(k, 2)), 8)
            lhs = jnp.concatenate([strips[h, s] for s in range(S)], axis=1)
            out = jnp.dot(lhs, first[t], preferred_element_type=F32)
            for pair in range(2):
                tile = out[:, 128 * pair : 128 * pair + 128]
                for half in range(2):
                    firsts = []
                    seconds = []
                    for gp in (2 * half, 2 * half + 1):
                        even = tile[16 * gp : 16 * gp + 8]
                        odd = tile[16 * gp + 8 : 16 * gp + 16]
                        firsts.append(jnp.where(left, even, pltpu.roll(odd, 64, 1)))
                        seconds.append(jnp.where(left, pltpu.roll(even, 64, 1), odd))
                    lines[h, 4 * t + 2 * pair, half] = jnp.concatenate(firsts, axis=0).astype(BF)
                    lines[h, 4 * t + 2 * pair + 1, half] = jnp.concatenate(seconds, axis=0).astype(BF)
            for i in range(4):
                to = 4 * t + i

                @pl.when(to != me)
                def _():
                    line_copy(h, to).start()

                @pl.when(to == me)
                def _():
                    line_local(h).start()

    def column_transform(h):
        line_local(h).wait()

        @pl.loop(1, B)
        def _(k):
            at = lax.rem(me + k, B)
            remote(
                lines.at[h, at], lrec.at[h, at], li_send.at[h, at], li_recv.at[h, at], (v, at // S, lax.rem(at, S))
            ).wait_recv()

        pieces = []
        for half in range(2):
            wide = lrec[h, :, half].astype(F32)
            for gp in range(2):
                pieces.append(wide[:, 8 * gp : 8 * gp + 8].reshape(256, 128).astype(BF))
        arrived = jnp.concatenate(pieces, axis=1)
        lhs = lax.dot_general(perm[...], arrived, (((1,), (1,)), ((), ())), preferred_element_type=F32).astype(BF)

        @pl.loop(0, 4)
        def _(t):
            lanes = pl.ds(pl.multiple_of(t * 256, 256), 256)
            spec[h, :, lanes] = jnp.dot(lhs, cols[h, :, lanes], preferred_element_type=F32)

    def gather_kernel_x():
        for copy in k2:
            copy.wait_recv()
        mine = pl.ds(4 * v, 4)
        for k in range(1, 4):
            remote(
                krec.at[mine], krec.at[mine], k_send.at[3 + k], k_recv.at[3 + k], (lax.rem(v + 2 * k, V), y, z)
            ).start()
        remote(krec.at[mine], krec.at[mine], k_send.at[8], k_recv.at[8], (sibling, y, z)).start()

    def k2_arrival(k):
        at = pl.ds(4 * lax.rem(v - 2 * k + V, V), 4)
        return remote(
            krec.at[at], krec.at[at], k_send.at[3 + k], k_recv.at[3 + k], (lax.rem(v + 2 * k, V), y, z)
        )

    def gather_kernel_core():
        for k in range(1, 4):
            k2_arrival(k).wait_recv()
            at = pl.ds(4 * lax.rem(v - 2 * k + V, V), 4)
            remote(krec.at[at], krec.at[at], k_send.at[8 + k], k_recv.at[8 + k], (sibling, y, z)).start()

    def k3_arrival(k):
        at = pl.ds(4 * lax.rem(sibling - 2 * k + V, V), 4)
        return remote(krec.at[at], krec.at[at], k_send.at[8 + k], k_recv.at[8 + k], (sibling, y, z))

    def rs_start(h):
        for copy in rs[h][:4]:
            copy.start()

    def rs_sent(h):
        for copy in rs[h]:
            copy.wait_send()

    thicknesses(0, op)
    rs[0][0].start()
    rs[0][1].start()
    thicknesses(1, op)
    rs[1][0].start()
    rs[1][1].start()
    thicknesses(0, up)
    thicknesses(0, dn)
    rs[0][2].start()
    rs[0][3].start()
    for copy in loads:
        copy.start()
    thicknesses(0, y)
    thicknesses(1, up)
    thicknesses(1, dn)
    thicknesses(1, y)
    thicknesses(2, op)
    rs_add(0)
    rs[1][2].start()
    rs[1][3].start()
    rs[2][0].start()
    rs[2][1].start()
    thicknesses(2, up)
    thicknesses(2, dn)
    thicknesses(3, op)
    rs_add(1)
    rs[2][2].start()
    rs[2][3].start()
    rs[3][0].start()
    rs[3][1].start()
    thicknesses(2, y)
    thicknesses(3, up)
    thicknesses(3, dn)
    thicknesses(3, y)
    make_source(0)
    rs_add(2)
    rs[3][2].start()
    rs[3][3].start()
    make_source(1)
    loads[0].wait()
    make_lines(0)
    rs_add(3)
    make_source(2)
    turn_kernel()
    make_lines(1)
    make_source(3)
    make_lines(2)
    gather_kernel_x()
    make_lines(3)
    loads[1].wait()
    loads[5].wait()
    loads[6].wait()
    column_transform(0)
    gather_kernel_core()
    column_transform(1)
    column_transform(2)
    column_transform(3)
    for k in range(4):
        k3_arrival(k).wait_recv()
    loads[2].wait()
    loads[3].wait()

    def mix(mp, special):
        rows = 16 * mp if special else pl.multiple_of(mp * 16, 16)
        slots = pl.ds(2 * mp, 2)

        def kernel_tile(ref_slice):
            return ref_slice.astype(F32).reshape(16, 128)

        if special:
            row = lax.broadcasted_iota(jnp.int32, (16, 128), 0)
            chosen = row + 8 * me < 8
        for u in range(F // 128):
            lanes = pl.ds(128 * u, 128)
            sins = pl.ds(F + 128 * u, 128)
            vals = []
            for rows_at in (pl.ds(rows, 16), pl.ds(256 + rows, 16)):
                cos = [spec[h, rows_at, lanes] for h in range(H)]
                sin = [spec[h, rows_at, sins] for h in range(H)]
                c0, c1, d0, d1 = cos[0] + cos[2], cos[0] - cos[2], cos[1] + cos[3], cos[1] - cos[3]
                s0, s1, t0, t1 = sin[0] + sin[2], sin[0] - sin[2], sin[1] + sin[3], sin[1] - sin[3]
                vals.append(
                    (
                        (c0 + d0, s0 + t0),
                        (c1 - t1, s1 + d1),
                        (c0 - d0, s0 - t0),
                        (c1 + t1, s1 - d1),
                    )
                )
            for k in range(H):
                (a, c), (b, d) = vals[0][k], vals[1][k]
                plus_r, plus_i = a + d, b - c
                minus_r, minus_i = a - d, b + c
                if special:
                    plus_r = jnp.where(chosen, a, plus_r)
                    plus_i = jnp.where(chosen, -c, plus_i)
                    minus_r = jnp.where(chosen, b, minus_r)
                    minus_i = jnp.where(chosen, d, minus_i)
                at = pl.ds(F * k + 128 * u, 128)
                kr = kernel_tile(kown[0, slots, :, at])
                ki = kernel_tile(kown[1, slots, :, at])
                lr = kernel_tile(krec[slots, 0, :, at])
                li = kernel_tile(krec[slots, 1, :, at])
                mr = kr * plus_r - ki * plus_i
                mi = kr * plus_i + ki * plus_r
                nr = lr * minus_r + li * minus_i
                ni = li * minus_r - lr * minus_i
                x1, x2, x3, x4 = mr + nr, mi + ni, mi - ni, mr - nr
                if special:
                    x1 = jnp.where(chosen, mr, x1)
                    x2 = jnp.where(chosen, mi, x2)
                    x3 = jnp.where(chosen, nr, x3)
                    x4 = jnp.where(chosen, -ni, x4)
                for i, x in enumerate((x1, x2, x3, x4)):
                    prod[i, pl.ds(rows, 16), at] = x.astype(BF)

    mix(0, True)

    @pl.loop(1, 16)
    def _(mp):
        mix(mp, False)

    sums = []
    for i in range(4):
        full = jnp.dot(ones[...], prod[i], preferred_element_type=F32) * SCALE
        sums.append([full[:, F * k : F * k + F] for k in range(H)])
    u1, u2, u3, u4 = sums

    def turned(h, one, other):
        total = one[0]
        for k in range(1, H):
            by = h * k % 4
            term = one[k] if by % 2 == 0 else other[k]
            total = total + term if by < 2 else total - term
        return total

    def negative(values):
        return [-value for value in values]

    sides = []
    for hh in range(2):
        total = None
        for hl in range(2):
            h = 2 * hh + hl
            real = [turned(h, u1, negative(u2)), turned(h, negative(u2), negative(u1))]
            imag = [turned(h, u3, u4), turned(h, u4, negative(u3))]
            wide = jnp.concatenate(
                [jnp.concatenate(real, axis=1), jnp.concatenate(imag, axis=1)], axis=0
            ).astype(BF)
            none = jnp.zeros_like(wide)
            wide = jnp.concatenate([wide, none] if hl == 0 else [none, wide], axis=0)
            one = lax.dot_general(cols[h], wide, (((1,), (1,)), ((), ())), preferred_element_type=F32)
            total = one if total is None else total + one
        sides.append(total.reshape(B, 8, 128))
    back[...] = jnp.concatenate(sides, axis=1).astype(BF)

    def back_copy(to):
        return remote(back.at[to], brec.at[me], ba_send.at[to], ba_recv.at[me], (v, to // S, lax.rem(to, S)))

    @pl.loop(1, B // 2)
    def _(k):
        back_copy(lax.rem(me + k, B)).start()
        back_copy(lax.rem(me + B - k, B)).start()

    back_copy(lax.rem(me + B // 2, B)).start()
    brec[me] = back[me]
    loads[4].wait()

    @pl.loop(1, B)
    def _(k):
        at = lax.rem(me + k, B)
        remote(back.at[at], brec.at[at], ba_send.at[at], ba_recv.at[at], (v, at // S, lax.rem(at, S))).wait_recv()

    even = []
    odd = []
    for dp in range(B // 2):
        b0 = brec[2 * dp].astype(F32)
        b1 = brec[2 * dp + 1].astype(F32)
        even.append(jnp.where(left16, b0, pltpu.roll(b1, 64, 1)).astype(BF))
        odd.append(jnp.where(left16, pltpu.roll(b0, 64, 1), b1).astype(BF))
    lhs = jnp.concatenate([jnp.concatenate(even, axis=1), jnp.concatenate(odd, axis=1)], axis=0)
    for t in range(4):
        lanes = pl.ds(256 * t, 256)
        image = jnp.dot(lhs, last[:, lanes], preferred_element_type=F32) * SCALE
        for half in range(2):
            tile = 2 * t + half
            for hl in range(2):
                for hh in range(2):
                    row = 16 * hl + 8 * hh
                    woven[tile, pl.ds(2 * hh + hl, 8, stride=H), :] = image[row : row + 8, 128 * half : 128 * half + 128]
            scat_ref[:, pl.ds(128 * tile, 128)] = woven[tile]

    for h in range(H):
        rs_sent(h)

        @pl.loop(1, S)
        def _(k):
            strip_copy(h, lax.rem(z + k, S)).wait_send()

        @pl.loop(1, B)
        def _(k):
            line_copy(h, lax.rem(me + k, B)).wait_send()

    for copy in k1[1:] + k2:
        copy.wait_send()

    @pl.when(v > 0)
    def _():
        k1[0].wait_send()

    for k in range(1, 4):
        k2_arrival(k).wait_send()
    for k in range(4):
        k3_arrival(k).wait_send()

    @pl.loop(1, B)
    def _(k):
        back_copy(lax.rem(me + k, B)).wait_send()


def finish_kernel(prim_in, scat_in, prim_out, scat_out):
    prim_out[...] = prim_in[...]
    scat_out[...] = scat_in[...]


def shards(attenuation, material, tilt, kernel_spectra):
    first, cols, last, perm, ones = (jnp.asarray(t) for t in tables())
    vmem = pl.BlockSpec(memory_space=pltpu.VMEM)
    hbm = pl.BlockSpec(memory_space=pl.ANY)
    dma = pltpu.SemaphoreType.DMA
    shapes = (jax.ShapeDtypeStruct((H * PART, 128), F32), jax.ShapeDtypeStruct((Q, N), F32))
    results = pl.pallas_call(
        main_kernel,
        out_shape=shapes,
        in_specs=[pl.BlockSpec(memory_space=pltpu.SMEM), hbm, hbm, hbm, hbm, hbm, hbm, hbm, hbm],
        out_specs=(vmem, vmem),
        scratch_shapes=[
            pltpu.VMEM((4, N, 128), BF),
            pltpu.VMEM((4, N + 2 * EDGE, 128), F32),
            pltpu.VMEM((4, N + 2 * EDGE, 128), jnp.int32),
            pltpu.VMEM((H, D, G, PART, 128), BF),
            pltpu.VMEM((8, N, 256), BF),
            pltpu.VMEM((H, N // H, 2 * F), BF),
            pltpu.VMEM((PAD, N), BF),
            pltpu.VMEM((512, 512), BF),
            pltpu.VMEM((Q, Q * G), BF),
            pltpu.VMEM((2, Q, G, PAD), BF),
            pltpu.VMEM((Q, 2, G, PAD), BF),
            pltpu.VMEM((4, 2, G, PAD), BF),
            pltpu.VMEM((H, 2, 4, PART, 128), BF),
            pltpu.VMEM((H, 2, 4, PART, 128), BF),
            pltpu.VMEM((H, G, PART, 128), BF),
            pltpu.VMEM((H, G, PART, 128), BF),
            pltpu.VMEM((H, S, 64, 128), BF),
            pltpu.VMEM((H, S, 64, 128), BF),
            pltpu.VMEM((H, B, 2, 16, 128), BF),
            pltpu.VMEM((H, B, 2, 16, 128), BF),
            pltpu.VMEM((H, 512, 2 * F), F32),
            pltpu.VMEM((4, Q * G, PAD), BF),
            pltpu.VMEM((B, 16, 128), BF),
            pltpu.VMEM((B, 16, 128), BF),
            pltpu.VMEM((8, Q, 128), F32),
            dma((4,)),
            dma((7,)),
            dma((H, 6)),
            dma((H, 6)),
            dma((H, S)),
            dma((H, S)),
            dma((H, B)),
            dma((H, B)),
            dma((B,)),
            dma((B,)),
            dma((16,)),
            dma((16,)),
        ],
        compiler_params=pltpu.CompilerParams(
            collective_id=0, has_side_effects=True, vmem_limit_bytes=60 * 2**20
        ),
        name="scatter",
    )(tilt, attenuation, material, kernel_spectra, first, cols, last, perm, ones)
    return pl.pallas_call(
        finish_kernel,
        out_shape=shapes,
        in_specs=[vmem, vmem],
        out_specs=(vmem, vmem),
        name="finish",
    )(*results)


def solution(mesh):
    return jax.shard_map(
        shards,
        mesh=mesh,
        in_specs=(
            P(("view", "depth"), None, "stripe"),
            P(("view", "depth"), None, "stripe"),
            P("view"),
            P(None, ("depth", "stripe"), None, None),
        ),
        out_specs=(P(("view", "depth"), "stripe"), P(("view", "depth", "stripe"), None)),
        check_vma=False,
    )
```

```python
import math

import jax
import jax.numpy as jnp
import ml_dtypes
import numpy as np
from jax import lax
from jax.experimental import pallas as pl
from jax.experimental.pallas import tpu as pltpu
from jax.sharding import PartitionSpec as P

G = 8
N = 1024
PAD = 2 * N
V, D, S = 8, 4, 8
B = D * S
Q = N // B
H = 4
PART = 64
F = PAD // H
EDGE = 64
BF = jnp.bfloat16
F32 = jnp.float32
MESH = pl.DeviceIdType.MESH
SCALE = 1.0 / PAD


def tables():
    d = np.arange(B)[:, None]
    m = np.arange(Q)[None, :]
    q = (64 * d + np.where((d >= B // 2) & (m == 0), 32, m)).reshape(-1)
    c = np.arange(N)
    angle = 2.0 * math.pi / PAD * (q[:, None] * c[None, :] % PAD)
    re = np.cos(angle)
    im = -np.sin(angle)
    im[0] = 1.0 - 2.0 * (c % 2)
    last = np.stack([re.reshape(B, Q, N), im.reshape(B, Q, N)], axis=1).reshape(2 * N, N)
    first = last.T.reshape(N, 8, 256).transpose(1, 0, 2)
    r = np.arange(N // H)
    p = np.arange(F)
    cols = []
    for h in range(H):
        angle = 2.0 * math.pi / PAD * ((H * r + h)[:, None] * p[None, :] % PAD)
        cols.append(np.concatenate([np.cos(angle), np.sin(angle)], axis=1))
    perm = np.zeros((2, Q, G, G, 2, Q))
    for x in range(2):
        for slot in range(Q):
            for g in range(G):
                perm[x, slot, g, g, x, slot] = 1.0
    perm = perm.reshape(512, 512)
    ones = np.kron(np.eye(Q), np.ones((1, G)))
    bf = ml_dtypes.bfloat16
    return tuple(np.ascontiguousarray(t).astype(bf) for t in (first, np.stack(cols), np.stack([c.T for c in cols]), last, perm, ones))


def main_kernel(
    tilt_ref,
    att_hbm,
    mat_hbm,
    k_hbm,
    first_hbm,
    cols_hbm,
    cols_t_hbm,
    last_hbm,
    perm_hbm,
    ones_hbm,
    prim_ref,
    scat_ref,
    att,
    att_ext,
    mat_ext,
    part,
    first,
    cols,
    cols_t,
    last,
    perm,
    ones,
    kown,
    krec,
    kmid,
    relay,
    partial,
    from_dn,
    from_up,
    source,
    strips,
    lines,
    lrec,
    spec,
    prod,
    back,
    brec,
    woven,
    plane_sem,
    load_sem,
    rs_send,
    rs_recv,
    st_send,
    st_recv,
    li_send,
    li_recv,
    ba_send,
    ba_recv,
    k_send,
    k_recv,
):
    v = lax.axis_index("view")
    y = lax.axis_index("depth")
    z = lax.axis_index("stripe")
    me = y * S + z
    high = me // 16
    up = lax.rem(y + 1, D)
    dn = lax.rem(y + 3, D)
    op = lax.rem(y + 2, D)
    sibling = v + 1 - 2 * lax.rem(v, 2)

    planes = [
        pltpu.make_async_copy(att_hbm, att, plane_sem.at[0]),
        pltpu.make_async_copy(mat_hbm, mat_ext.at[:, pl.ds(EDGE, N)], plane_sem.at[1]),
        pltpu.make_async_copy(mat_hbm.at[:, pl.ds(N - EDGE, EDGE)], mat_ext.at[:, pl.ds(0, EDGE)], plane_sem.at[2]),
        pltpu.make_async_copy(mat_hbm.at[:, pl.ds(0, EDGE)], mat_ext.at[:, pl.ds(EDGE + N, EDGE)], plane_sem.at[3]),
    ]
    for copy in planes:
        copy.start()
    loads = [
        pltpu.make_async_copy(first_hbm, first, load_sem.at[0]),
        pltpu.make_async_copy(cols_hbm, cols, load_sem.at[1]),
        pltpu.make_async_copy(k_hbm.at[:, pl.ds(1, Q - 1)], kown.at[:, pl.ds(1, Q - 1)], load_sem.at[2]),
        pltpu.make_async_copy(k_hbm.at[:, pl.ds(32 * high, 1)], kown.at[:, pl.ds(0, 1)], load_sem.at[3]),
        pltpu.make_async_copy(last_hbm, last, load_sem.at[4]),
        pltpu.make_async_copy(perm_hbm, perm, load_sem.at[5]),
        pltpu.make_async_copy(ones_hbm, ones, load_sem.at[6]),
        pltpu.make_async_copy(cols_t_hbm, cols_t, load_sem.at[7]),
    ]

    barrier = pltpu.get_barrier_semaphore()

    @pl.loop(1, B)
    def _(k):
        to = lax.rem(me + k, B)
        pl.semaphore_signal(barrier, inc=1, device_id=(v, to // S, lax.rem(to, S)), device_id_type=MESH)

    for k in range(1, 4):
        pl.semaphore_signal(barrier, inc=1, device_id=(lax.rem(v + 2 * k, V), y, z), device_id_type=MESH)
    pl.semaphore_signal(barrier, inc=1, device_id=(sibling, y, z), device_id_type=MESH)

    pl.semaphore_wait(barrier, B - 1 + 4)
    def remote(src, dst, send, recv, to):
        return pltpu.make_async_remote_copy(
            src_ref=src, dst_ref=dst, send_sem=send, recv_sem=recv, device_id=to, device_id_type=MESH
        )

    lo, hi = pl.ds(0, 4), pl.ds(4, 4)
    to_up, to_dn = (v, up, z), (v, dn, z)

    def rs_copies(h):
        return [
            remote(part.at[h, op, lo], relay.at[h, 0], rs_send.at[h, 0], rs_recv.at[h, 0], to_up),
            remote(part.at[h, op, hi], relay.at[h, 1], rs_send.at[h, 1], rs_recv.at[h, 1], to_dn),
            remote(part.at[h, up, hi], from_dn.at[h, hi], rs_send.at[h, 2], rs_recv.at[h, 2], to_up),
            remote(part.at[h, dn, lo], from_up.at[h, lo], rs_send.at[h, 3], rs_recv.at[h, 3], to_dn),
            remote(partial.at[h, 0], from_dn.at[h, lo], rs_send.at[h, 4], rs_recv.at[h, 4], to_up),
            remote(partial.at[h, 1], from_up.at[h, hi], rs_send.at[h, 5], rs_recv.at[h, 5], to_dn),
        ]

    rs = [rs_copies(h) for h in range(H)]
    across = (v, y, S - 1 - z)
    over = (v, D - 1 - y, z)
    k1 = []
    k2 = []
    for i in range(4):
        pos = 32 + lax.rem(32 - (4 * v + i), 32)
        k1.append(remote(k_hbm.at[:, pos], kmid.at[i], k_send.at[12 + i], k_recv.at[12 + i], across))
        k2.append(remote(kmid.at[i], krec.at[4 * v + i], k_send.at[i], k_recv.at[i], over))
    single = (B - 1 - me) * (1 - high) + lax.rem(64 - me, 16) * high
    k_single = remote(
        k_hbm.at[:, 32 * (1 - high)], krec.at[0], k_send.at[0], k_recv.at[0], (v, single // S, lax.rem(single, S))
    )
    def fetch_kernel():
        for copy in k1[1:]:
            copy.start()

        @pl.when(v == 0)
        def _():
            k_single.start()

        @pl.when(v > 0)
        def _():
            k1[0].start()

    fetch_kernel()
    planes[0].wait()
    for plane in range(4):

        @pl.loop(0, N // 128)
        def _(i):
            row = pl.multiple_of(i * 128, 128)
            att_ext[plane, pl.ds(row + EDGE, 128), :] = att[plane, pl.ds(row, 128), :].astype(F32)

        att_ext[plane, pl.ds(0, EDGE), :] = att[plane, pl.ds(N - EDGE, EDGE), :].astype(F32)
        att_ext[plane, pl.ds(EDGE + N, EDGE), :] = att[plane, pl.ds(0, EDGE), :].astype(F32)
    for copy in planes[1:]:
        copy.wait()
    shear = tilt_ref[0]

    def thicknesses(h, j):
        @pl.loop(0, 2, unroll=2)
        def _(c):
            start = EDGE + 256 * j + 128 * c + h
            dens = []
            kind = []
            for plane in range(4):
                at = start - shear * (4 * y + plane)
                dens.append(att_ext[plane, pl.ds(at, 32, stride=H), :])
                kind.append(mat_ext[plane, pl.ds(at, 32, stride=H), :])
            for g in range(G):
                acc = jnp.where(kind[0] == g, dens[0], 0.0)
                for plane in range(1, 4):
                    acc = acc + jnp.where(kind[plane] == g, dens[plane], 0.0)
                part[h, j, g, pl.ds(pl.multiple_of(c * 32, 32), 32), :] = acc.astype(BF)

    def turn_kernel():
        for i in range(1, 4):
            k1[i].wait_recv()
            k2[i].start()

        @pl.when(v > 0)
        def _():
            k1[0].wait_recv()
            k2[0].start()

    def rs_add(h):
        for way, group in ((0, lo), (1, hi)):
            rs[h][way].wait_recv()
            block = up if way == 0 else dn

            for g in range(4):
                mine = part[h, block, 4 * way + g].astype(F32)
                partial[h, way, g] = (mine + relay[h, way, g].astype(F32)).astype(BF)
            rs[h][4 + way].start()

    def strip_copy(h, to):
        return remote(source.at[h, to], strips.at[h, z], st_send.at[h, to], st_recv.at[h, z], (v, y, to))

    def make_source(h):
        for i in range(2, 6):
            rs[h][i].wait_recv()

        for k in range(S // 2):
            pair = lax.rem(z // 2 + 1 + k, S // 2)
            row = pl.multiple_of(pair * 16, 16)
            rows = pl.ds(row, 16)
            thick = []
            for g in range(G):
                thick.append(
                    part[h, y, g, rows, :].astype(F32)
                    + from_dn[h, g, rows, :].astype(F32)
                    + from_up[h, g, rows, :].astype(F32)
                )
            total = thick[0]
            for g in range(1, G):
                total = total + thick[g]
            prim = jnp.exp(-total)
            prim_ref[pl.ds(H * row + h, 16, stride=H), :] = prim
            values = [prim * thick[g] for g in range(G)]
            for side in range(2):
                to = 2 * pair + side
                cut = slice(8 * side, 8 * side + 8)
                for gp in range(G // 2):
                    both = jnp.concatenate([values[2 * gp][cut], values[2 * gp + 1][cut]], axis=0)
                    source[h, to, pl.ds(16 * gp, 16), :] = both.astype(BF)

                @pl.when(to != z)
                def _():
                    strip_copy(h, to).start()

        strips[h, z] = source[h, z]

    left = lax.broadcasted_iota(jnp.int32, (8, 128), 1) < 64
    left16 = lax.broadcasted_iota(jnp.int32, (16, 128), 1) < 64

    def line_copy(h, to):
        return remote(lines.at[h, to], lrec.at[h, me], li_send.at[h, to], li_recv.at[h, me], (v, to // S, lax.rem(to, S)))

    def line_local(h):
        return pltpu.make_async_copy(lines.at[h, me], lrec.at[h, me], li_recv.at[h, me])

    def make_lines(h):
        @pl.loop(1, S)
        def _(k):
            at = lax.rem(z + k, S)
            remote(source.at[h, at], strips.at[h, at], st_send.at[h, at], st_recv.at[h, at], (v, y, at)).wait_recv()

        @pl.loop(0, 8)
        def _(k):
            step = (k + 1) // 2
            t = lax.rem(me // 4 + 8 + step * (1 - 2 * lax.rem(k, 2)), 8)
            lhs = jnp.concatenate([strips[h, s] for s in range(S)], axis=1)
            out = jnp.dot(lhs, first[t], preferred_element_type=F32)
            for pair in range(2):
                tile = out[:, 128 * pair : 128 * pair + 128]
                for half in range(2):
                    firsts = []
                    seconds = []
                    for gp in (2 * half, 2 * half + 1):
                        even = tile[16 * gp : 16 * gp + 8]
                        odd = tile[16 * gp + 8 : 16 * gp + 16]
                        firsts.append(jnp.where(left, even, pltpu.roll(odd, 64, 1)))
                        seconds.append(jnp.where(left, pltpu.roll(even, 64, 1), odd))
                    lines[h, 4 * t + 2 * pair, half] = jnp.concatenate(firsts, axis=0).astype(BF)
                    lines[h, 4 * t + 2 * pair + 1, half] = jnp.concatenate(seconds, axis=0).astype(BF)
            for i in range(4):
                to = 4 * t + i

                @pl.when(to != me)
                def _():
                    line_copy(h, to).start()

                @pl.when(to == me)
                def _():
                    line_local(h).start()

    def column_transform(h):
        line_local(h).wait()

        @pl.loop(1, B)
        def _(k):
            at = lax.rem(me + k, B)
            remote(
                lines.at[h, at], lrec.at[h, at], li_send.at[h, at], li_recv.at[h, at], (v, at // S, lax.rem(at, S))
            ).wait_recv()

        pieces = []
        for half in range(2):
            wide = lrec[h, :, half].astype(F32)
            for gp in range(2):
                pieces.append(wide[:, 8 * gp : 8 * gp + 8].reshape(256, 128).astype(BF))
        arrived = jnp.concatenate(pieces, axis=1)
        lhs = lax.dot_general(perm[...], arrived, (((1,), (1,)), ((), ())), preferred_element_type=F32).astype(BF)

        @pl.loop(0, 4, unroll=4)
        def _(t):
            lanes = pl.ds(pl.multiple_of(t * 256, 256), 256)
            spec[h, :, lanes] = jnp.dot(lhs, cols[h, :, lanes], preferred_element_type=F32)

    def gather_kernel_x():
        for copy in k2:
            copy.wait_recv()
        mine = pl.ds(4 * v, 4)
        for k in range(1, 4):
            remote(
                krec.at[mine], krec.at[mine], k_send.at[3 + k], k_recv.at[3 + k], (lax.rem(v + 2 * k, V), y, z)
            ).start()
        remote(krec.at[mine], krec.at[mine], k_send.at[8], k_recv.at[8], (sibling, y, z)).start()

    def k2_arrival(k):
        at = pl.ds(4 * lax.rem(v - 2 * k + V, V), 4)
        return remote(
            krec.at[at], krec.at[at], k_send.at[3 + k], k_recv.at[3 + k], (lax.rem(v + 2 * k, V), y, z)
        )

    def gather_kernel_core():
        for k in range(1, 4):
            k2_arrival(k).wait_recv()
            at = pl.ds(4 * lax.rem(v - 2 * k + V, V), 4)
            remote(krec.at[at], krec.at[at], k_send.at[8 + k], k_recv.at[8 + k], (sibling, y, z)).start()

    def k3_arrival(k):
        at = pl.ds(4 * lax.rem(sibling - 2 * k + V, V), 4)
        return remote(krec.at[at], krec.at[at], k_send.at[8 + k], k_recv.at[8 + k], (sibling, y, z))

    def rs_start(h):
        for copy in rs[h][:4]:
            copy.start()

    def rs_sent(h):
        for copy in rs[h]:
            copy.wait_send()

    thicknesses(0, op)
    rs[0][0].start()
    rs[0][1].start()
    thicknesses(1, op)
    rs[1][0].start()
    rs[1][1].start()
    thicknesses(0, up)
    thicknesses(0, dn)
    rs[0][2].start()
    rs[0][3].start()
    for copy in loads:
        copy.start()
    thicknesses(0, y)
    thicknesses(1, up)
    thicknesses(1, dn)
    thicknesses(1, y)
    thicknesses(2, op)
    rs_add(0)
    rs[1][2].start()
    rs[1][3].start()
    rs[2][0].start()
    rs[2][1].start()
    thicknesses(2, up)
    thicknesses(2, dn)
    thicknesses(3, op)
    rs_add(1)
    rs[2][2].start()
    rs[2][3].start()
    rs[3][0].start()
    rs[3][1].start()
    thicknesses(2, y)
    thicknesses(3, up)
    thicknesses(3, dn)
    thicknesses(3, y)
    make_source(0)
    rs_add(2)
    rs[3][2].start()
    rs[3][3].start()
    make_source(1)
    loads[0].wait()
    make_lines(0)
    rs_add(3)
    make_source(2)
    turn_kernel()
    make_lines(1)
    make_source(3)
    make_lines(2)
    gather_kernel_x()
    make_lines(3)
    loads[1].wait()
    loads[5].wait()
    loads[6].wait()
    loads[7].wait()
    column_transform(0)
    gather_kernel_core()
    column_transform(1)
    column_transform(2)
    column_transform(3)
    for k in range(4):
        k3_arrival(k).wait_recv()
    loads[2].wait()
    loads[3].wait()

    def mix(mp, special):
        rows = 16 * mp if special else pl.multiple_of(mp * 16, 16)
        slots = pl.ds(2 * mp, 2)

        def kernel_tile(ref_slice):
            return ref_slice.astype(F32).reshape(16, 128)

        if special:
            row = lax.broadcasted_iota(jnp.int32, (16, 128), 0)
            chosen = row + 8 * me < 8
        for u in range(F // 128):
            lanes = pl.ds(128 * u, 128)
            sins = pl.ds(F + 128 * u, 128)
            vals = []
            for rows_at in (pl.ds(rows, 16), pl.ds(256 + rows, 16)):
                cos = [spec[h, rows_at, lanes] for h in range(H)]
                sin = [spec[h, rows_at, sins] for h in range(H)]
                c0, c1, d0, d1 = cos[0] + cos[2], cos[0] - cos[2], cos[1] + cos[3], cos[1] - cos[3]
                s0, s1, t0, t1 = sin[0] + sin[2], sin[0] - sin[2], sin[1] + sin[3], sin[1] - sin[3]
                vals.append(
                    (
                        (c0 + d0, s0 + t0),
                        (c1 - t1, s1 + d1),
                        (c0 - d0, s0 - t0),
                        (c1 + t1, s1 - d1),
                    )
                )
            for k in range(H):
                (a, c), (b, d) = vals[0][k], vals[1][k]
                plus_r, plus_i = a + d, b - c
                minus_r, minus_i = a - d, b + c
                if special:
                    plus_r = jnp.where(chosen, a, plus_r)
                    plus_i = jnp.where(chosen, -c, plus_i)
                    minus_r = jnp.where(chosen, b, minus_r)
                    minus_i = jnp.where(chosen, d, minus_i)
                at = pl.ds(F * k + 128 * u, 128)
                kr = kernel_tile(kown[0, slots, :, at])
                ki = kernel_tile(kown[1, slots, :, at])
                lr = kernel_tile(krec[slots, 0, :, at])
                li = kernel_tile(krec[slots, 1, :, at])
                mr = kr * plus_r - ki * plus_i
                mi = kr * plus_i + ki * plus_r
                nr = lr * minus_r + li * minus_i
                ni = li * minus_r - lr * minus_i
                x1, x2, x3, x4 = mr + nr, mi + ni, mi - ni, mr - nr
                if special:
                    x1 = jnp.where(chosen, mr, x1)
                    x2 = jnp.where(chosen, mi, x2)
                    x3 = jnp.where(chosen, nr, x3)
                    x4 = jnp.where(chosen, -ni, x4)
                for i, x in enumerate((x1, x2, x3, x4)):
                    prod[i, pl.ds(rows, 16), at] = x.astype(BF)

    mix(0, True)

    @pl.loop(1, 16, unroll=3)
    def _(mp):
        mix(mp, False)

    sums = []
    for i in range(4):
        full = jnp.dot(ones[...], prod[i], preferred_element_type=F32) * SCALE
        sums.append([full[:, F * k : F * k + F] for k in range(H)])
    u1, u2, u3, u4 = sums

    def turned(h, one, other):
        total = one[0]
        for k in range(1, H):
            by = h * k % 4
            term = one[k] if by % 2 == 0 else other[k]
            total = total + term if by < 2 else total - term
        return total

    def negative(values):
        return [-value for value in values]

    sides = []
    for hh in range(2):
        both = []
        for h in (2 * hh, 2 * hh + 1):
            real = [turned(h, u1, negative(u2)), turned(h, negative(u2), negative(u1))]
            imag = [turned(h, u3, u4), turned(h, u4, negative(u3))]
            wide = jnp.concatenate(
                [jnp.concatenate(real, axis=1), jnp.concatenate(imag, axis=1)], axis=0
            ).astype(BF)
            both.append(jnp.dot(wide, cols_t[h], preferred_element_type=F32))
        sides.append(jnp.concatenate(both, axis=0).T.reshape(B, 8, 128))
    back[...] = jnp.concatenate(sides, axis=1).astype(BF)

    def back_copy(to):
        return remote(back.at[to], brec.at[me], ba_send.at[to], ba_recv.at[me], (v, to // S, lax.rem(to, S)))

    @pl.loop(1, B // 2)
    def _(k):
        back_copy(lax.rem(me + k, B)).start()
        back_copy(lax.rem(me + B - k, B)).start()

    back_copy(lax.rem(me + B // 2, B)).start()
    brec[me] = back[me]
    loads[4].wait()

    @pl.loop(1, B)
    def _(k):
        at = lax.rem(me + k, B)
        remote(back.at[at], brec.at[at], ba_send.at[at], ba_recv.at[at], (v, at // S, lax.rem(at, S))).wait_recv()

    even = []
    odd = []
    for dp in range(B // 2):
        b0 = brec[2 * dp].astype(F32)
        b1 = brec[2 * dp + 1].astype(F32)
        even.append(jnp.where(left16, b0, pltpu.roll(b1, 64, 1)).astype(BF))
        odd.append(jnp.where(left16, pltpu.roll(b0, 64, 1), b1).astype(BF))
    lhs = jnp.concatenate([jnp.concatenate(even, axis=1), jnp.concatenate(odd, axis=1)], axis=0)
    for t in range(4):
        lanes = pl.ds(256 * t, 256)
        image = jnp.dot(lhs, last[:, lanes], preferred_element_type=F32) * SCALE
        for half in range(2):
            tile = 2 * t + half
            for hl in range(2):
                for hh in range(2):
                    row = 16 * hl + 8 * hh
                    woven[tile, pl.ds(2 * hh + hl, 8, stride=H), :] = image[row : row + 8, 128 * half : 128 * half + 128]
            scat_ref[:, pl.ds(128 * tile, 128)] = woven[tile]

    for h in range(H):
        rs_sent(h)

        @pl.loop(1, S)
        def _(k):
            strip_copy(h, lax.rem(z + k, S)).wait_send()

        @pl.loop(1, B)
        def _(k):
            line_copy(h, lax.rem(me + k, B)).wait_send()

    for copy in k1[1:] + k2:
        copy.wait_send()

    @pl.when(v > 0)
    def _():
        k1[0].wait_send()

    for k in range(1, 4):
        k2_arrival(k).wait_send()
    for k in range(4):
        k3_arrival(k).wait_send()

    @pl.loop(1, B)
    def _(k):
        back_copy(lax.rem(me + k, B)).wait_send()


def finish_kernel(prim_in, scat_in, prim_out, scat_out):
    prim_out[...] = prim_in[...]
    scat_out[...] = scat_in[...]


def shards(attenuation, material, tilt, kernel_spectra):
    first, cols, cols_t, last, perm, ones = (jnp.asarray(t) for t in tables())
    vmem = pl.BlockSpec(memory_space=pltpu.VMEM)
    hbm = pl.BlockSpec(memory_space=pl.ANY)
    dma = pltpu.SemaphoreType.DMA
    shapes = (jax.ShapeDtypeStruct((H * PART, 128), F32), jax.ShapeDtypeStruct((Q, N), F32))
    results = pl.pallas_call(
        main_kernel,
        out_shape=shapes,
        in_specs=[pl.BlockSpec(memory_space=pltpu.SMEM), hbm, hbm, hbm, hbm, hbm, hbm, hbm, hbm, hbm],
        out_specs=(vmem, vmem),
        scratch_shapes=[
            pltpu.VMEM((4, N, 128), BF),
            pltpu.VMEM((4, N + 2 * EDGE, 128), F32),
            pltpu.VMEM((4, N + 2 * EDGE, 128), jnp.int32),
            pltpu.VMEM((H, D, G, PART, 128), BF),
            pltpu.VMEM((8, N, 256), BF),
            pltpu.VMEM((H, N // H, 2 * F), BF),
            pltpu.VMEM((H, 2 * F, N // H), BF),
            pltpu.VMEM((PAD, N), BF),
            pltpu.VMEM((512, 512), BF),
            pltpu.VMEM((Q, Q * G), BF),
            pltpu.VMEM((2, Q, G, PAD), BF),
            pltpu.VMEM((Q, 2, G, PAD), BF),
            pltpu.VMEM((4, 2, G, PAD), BF),
            pltpu.VMEM((H, 2, 4, PART, 128), BF),
            pltpu.VMEM((H, 2, 4, PART, 128), BF),
            pltpu.VMEM((H, G, PART, 128), BF),
            pltpu.VMEM((H, G, PART, 128), BF),
            pltpu.VMEM((H, S, 64, 128), BF),
            pltpu.VMEM((H, S, 64, 128), BF),
            pltpu.VMEM((H, B, 2, 16, 128), BF),
            pltpu.VMEM((H, B, 2, 16, 128), BF),
            pltpu.VMEM((H, 512, 2 * F), F32),
            pltpu.VMEM((4, Q * G, PAD), BF),
            pltpu.VMEM((B, 16, 128), BF),
            pltpu.VMEM((B, 16, 128), BF),
            pltpu.VMEM((8, Q, 128), F32),
            dma((4,)),
            dma((8,)),
            dma((H, 6)),
            dma((H, 6)),
            dma((H, S)),
            dma((H, S)),
            dma((H, B)),
            dma((H, B)),
            dma((B,)),
            dma((B,)),
            dma((16,)),
            dma((16,)),
        ],
        compiler_params=pltpu.CompilerParams(
            collective_id=0, has_side_effects=True, vmem_limit_bytes=60 * 2**20
        ),
        name="scatter",
    )(tilt, attenuation, material, kernel_spectra, first, cols, cols_t, last, perm, ones)
    return pl.pallas_call(
        finish_kernel,
        out_shape=shapes,
        in_specs=[vmem, vmem],
        out_specs=(vmem, vmem),
        name="finish",
    )(*results)


def solution(mesh):
    return jax.shard_map(
        shards,
        mesh=mesh,
        in_specs=(
            P(("view", "depth"), None, "stripe"),
            P(("view", "depth"), None, "stripe"),
            P("view"),
            P(None, ("depth", "stripe"), None, None),
        ),
        out_specs=(P(("view", "depth"), "stripe"), P(("view", "depth", "stripe"), None)),
        check_vma=False,
    )
```

```python
import math

import jax
import jax.numpy as jnp
import ml_dtypes
import numpy as np
from jax import lax
from jax.experimental import pallas as pl
from jax.experimental.pallas import tpu as pltpu
from jax.sharding import PartitionSpec as P

G = 8
N = 1024
PAD = 2 * N
V, D, S = 8, 4, 8
B = D * S
Q = N // B
H = 4
PART = 64
F = PAD // H
EDGE = 64
BF = jnp.bfloat16
F32 = jnp.float32
MESH = pl.DeviceIdType.MESH
SCALE = 1.0 / PAD


def tables():
    d = np.arange(B)[:, None]
    m = np.arange(Q)[None, :]
    q = (64 * d + np.where((d >= B // 2) & (m == 0), 32, m)).reshape(-1)
    c = np.arange(N)
    angle = 2.0 * math.pi / PAD * (q[:, None] * c[None, :] % PAD)
    re = np.cos(angle)
    im = -np.sin(angle)
    im[0] = 1.0 - 2.0 * (c % 2)
    last = np.stack([re.reshape(B, Q, N), im.reshape(B, Q, N)], axis=1).reshape(2 * N, N)
    first = last.T.reshape(N, 8, 256).transpose(1, 0, 2)
    r = np.arange(N // H)
    p = np.arange(F)
    cols = []
    for h in range(H):
        angle = 2.0 * math.pi / PAD * ((H * r + h)[:, None] * p[None, :] % PAD)
        cols.append(np.concatenate([np.cos(angle), np.sin(angle)], axis=1))
    perm = np.zeros((2, Q, G, G, 2, Q))
    for x in range(2):
        for slot in range(Q):
            for g in range(G):
                perm[x, slot, g, g, x, slot] = 1.0
    perm = perm.reshape(512, 512)
    ones = np.kron(np.eye(Q), np.ones((1, G)))
    bf = ml_dtypes.bfloat16
    return tuple(np.ascontiguousarray(t).astype(bf) for t in (first, np.stack(cols), np.stack([c.T for c in cols]), last, perm, ones))


def main_kernel(
    tilt_ref,
    att_hbm,
    mat_hbm,
    k_hbm,
    first_hbm,
    cols_hbm,
    cols_t_hbm,
    last_hbm,
    perm_hbm,
    ones_hbm,
    prim_ref,
    scat_ref,
    att,
    att_ext,
    mat_ext,
    part,
    first,
    cols,
    cols_t,
    last,
    perm,
    ones,
    kown,
    krec,
    kmid,
    relay,
    partial,
    from_dn,
    from_up,
    source,
    strips,
    lines,
    lrec,
    spec,
    prod,
    back,
    brec,
    woven,
    plane_sem,
    load_sem,
    rs_send,
    rs_recv,
    st_send,
    st_recv,
    li_send,
    li_recv,
    ba_send,
    ba_recv,
    k_send,
    k_recv,
):
    v = lax.axis_index("view")
    y = lax.axis_index("depth")
    z = lax.axis_index("stripe")
    me = y * S + z
    high = me // 16
    up = lax.rem(y + 1, D)
    dn = lax.rem(y + 3, D)
    op = lax.rem(y + 2, D)
    sibling = v + 1 - 2 * lax.rem(v, 2)

    planes = [
        pltpu.make_async_copy(att_hbm, att, plane_sem.at[0]),
        pltpu.make_async_copy(mat_hbm, mat_ext.at[:, pl.ds(EDGE, N)], plane_sem.at[1]),
        pltpu.make_async_copy(mat_hbm.at[:, pl.ds(N - EDGE, EDGE)], mat_ext.at[:, pl.ds(0, EDGE)], plane_sem.at[2]),
        pltpu.make_async_copy(mat_hbm.at[:, pl.ds(0, EDGE)], mat_ext.at[:, pl.ds(EDGE + N, EDGE)], plane_sem.at[3]),
    ]
    for copy in planes:
        copy.start()
    loads = [
        pltpu.make_async_copy(first_hbm, first, load_sem.at[0]),
        pltpu.make_async_copy(cols_hbm, cols, load_sem.at[1]),
        pltpu.make_async_copy(k_hbm.at[:, pl.ds(1, Q - 1)], kown.at[:, pl.ds(1, Q - 1)], load_sem.at[2]),
        pltpu.make_async_copy(k_hbm.at[:, pl.ds(32 * high, 1)], kown.at[:, pl.ds(0, 1)], load_sem.at[3]),
        pltpu.make_async_copy(last_hbm, last, load_sem.at[4]),
        pltpu.make_async_copy(perm_hbm, perm, load_sem.at[5]),
        pltpu.make_async_copy(ones_hbm, ones, load_sem.at[6]),
        pltpu.make_async_copy(cols_t_hbm, cols_t, load_sem.at[7]),
    ]

    barrier = pltpu.get_barrier_semaphore()

    @pl.loop(1, B)
    def _(k):
        to = lax.rem(me + k, B)
        pl.semaphore_signal(barrier, inc=1, device_id=(v, to // S, lax.rem(to, S)), device_id_type=MESH)

    for k in range(1, 4):
        pl.semaphore_signal(barrier, inc=1, device_id=(lax.rem(v + 2 * k, V), y, z), device_id_type=MESH)
    pl.semaphore_signal(barrier, inc=1, device_id=(sibling, y, z), device_id_type=MESH)

    pl.semaphore_wait(barrier, B - 1 + 4)
    def remote(src, dst, send, recv, to):
        return pltpu.make_async_remote_copy(
            src_ref=src, dst_ref=dst, send_sem=send, recv_sem=recv, device_id=to, device_id_type=MESH
        )

    lo, hi = pl.ds(0, 4), pl.ds(4, 4)
    to_up, to_dn = (v, up, z), (v, dn, z)

    def rs_copies(h):
        return [
            remote(part.at[h, op, lo], relay.at[h, 0], rs_send.at[h, 0], rs_recv.at[h, 0], to_up),
            remote(part.at[h, op, hi], relay.at[h, 1], rs_send.at[h, 1], rs_recv.at[h, 1], to_dn),
            remote(part.at[h, up, hi], from_dn.at[h, hi], rs_send.at[h, 2], rs_recv.at[h, 2], to_up),
            remote(part.at[h, dn, lo], from_up.at[h, lo], rs_send.at[h, 3], rs_recv.at[h, 3], to_dn),
            remote(partial.at[h, 0], from_dn.at[h, lo], rs_send.at[h, 4], rs_recv.at[h, 4], to_up),
            remote(partial.at[h, 1], from_up.at[h, hi], rs_send.at[h, 5], rs_recv.at[h, 5], to_dn),
        ]

    rs = [rs_copies(h) for h in range(H)]
    across = (v, y, S - 1 - z)
    over = (v, D - 1 - y, z)
    k1 = []
    k2 = []
    for i in range(4):
        pos = 32 + lax.rem(32 - (4 * v + i), 32)
        k1.append(remote(k_hbm.at[:, pos], kmid.at[i], k_send.at[12 + i], k_recv.at[12 + i], across))
        k2.append(remote(kmid.at[i], krec.at[4 * v + i], k_send.at[i], k_recv.at[i], over))
    single = (B - 1 - me) * (1 - high) + lax.rem(64 - me, 16) * high
    k_single = remote(
        k_hbm.at[:, 32 * (1 - high)], krec.at[0], k_send.at[0], k_recv.at[0], (v, single // S, lax.rem(single, S))
    )
    def fetch_kernel():
        for copy in k1[1:]:
            copy.start()

        @pl.when(v == 0)
        def _():
            k_single.start()

        @pl.when(v > 0)
        def _():
            k1[0].start()

    fetch_kernel()
    planes[0].wait()
    for plane in range(4):

        @pl.loop(0, N // 128)
        def _(i):
            row = pl.multiple_of(i * 128, 128)
            att_ext[plane, pl.ds(row + EDGE, 128), :] = att[plane, pl.ds(row, 128), :].astype(F32)

        att_ext[plane, pl.ds(0, EDGE), :] = att[plane, pl.ds(N - EDGE, EDGE), :].astype(F32)
        att_ext[plane, pl.ds(EDGE + N, EDGE), :] = att[plane, pl.ds(0, EDGE), :].astype(F32)
    for copy in planes[1:]:
        copy.wait()
    shear = tilt_ref[0]

    def thicknesses(h, j):
        @pl.loop(0, 2, unroll=2)
        def _(c):
            start = EDGE + 256 * j + 128 * c + h
            dens = []
            kind = []
            for plane in range(4):
                at = start - shear * (4 * y + plane)
                dens.append(att_ext[plane, pl.ds(at, 32, stride=H), :])
                kind.append(mat_ext[plane, pl.ds(at, 32, stride=H), :])
            for g in range(G):
                acc = jnp.where(kind[0] == g, dens[0], 0.0)
                for plane in range(1, 4):
                    acc = acc + jnp.where(kind[plane] == g, dens[plane], 0.0)
                part[h, j, g, pl.ds(pl.multiple_of(c * 32, 32), 32), :] = acc.astype(BF)

    def turn_kernel():
        for i in range(1, 4):
            k1[i].wait_recv()
            k2[i].start()

        @pl.when(v > 0)
        def _():
            k1[0].wait_recv()
            k2[0].start()

    def rs_add(h):
        for way, group in ((0, lo), (1, hi)):
            rs[h][way].wait_recv()
            block = up if way == 0 else dn

            for g in range(4):
                mine = part[h, block, 4 * way + g].astype(F32)
                partial[h, way, g] = (mine + relay[h, way, g].astype(F32)).astype(BF)
            rs[h][4 + way].start()

    def strip_copy(h, to):
        return remote(source.at[h, to], strips.at[h, z], st_send.at[h, to], st_recv.at[h, z], (v, y, to))

    def make_source(h):
        for i in range(2, 6):
            rs[h][i].wait_recv()

        for k in range(S // 2):
            pair = lax.rem(z // 2 + 1 + k, S // 2)
            row = pl.multiple_of(pair * 16, 16)
            rows = pl.ds(row, 16)
            thick = []
            for g in range(G):
                thick.append(
                    part[h, y, g, rows, :].astype(F32)
                    + from_dn[h, g, rows, :].astype(F32)
                    + from_up[h, g, rows, :].astype(F32)
                )
            total = thick[0]
            for g in range(1, G):
                total = total + thick[g]
            prim = jnp.exp(-total)
            prim_ref[pl.ds(H * row + h, 16, stride=H), :] = prim
            values = [prim * thick[g] for g in range(G)]
            for side in range(2):
                to = 2 * pair + side
                cut = slice(8 * side, 8 * side + 8)
                for gp in range(G // 2):
                    both = jnp.concatenate([values[2 * gp][cut], values[2 * gp + 1][cut]], axis=0)
                    source[h, to, pl.ds(16 * gp, 16), :] = both.astype(BF)

                @pl.when(to != z)
                def _():
                    strip_copy(h, to).start()

        strips[h, z] = source[h, z]

    left = lax.broadcasted_iota(jnp.int32, (8, 128), 1) < 64
    left16 = lax.broadcasted_iota(jnp.int32, (16, 128), 1) < 64

    def line_copy(h, to):
        return remote(lines.at[h, to], lrec.at[h, me], li_send.at[h, to], li_recv.at[h, me], (v, to // S, lax.rem(to, S)))

    def line_local(h):
        return pltpu.make_async_copy(lines.at[h, me], lrec.at[h, me], li_recv.at[h, me])

    def make_lines(h):
        @pl.loop(1, S)
        def _(k):
            at = lax.rem(z + k, S)
            remote(source.at[h, at], strips.at[h, at], st_send.at[h, at], st_recv.at[h, at], (v, y, at)).wait_recv()

        @pl.loop(0, 8)
        def _(k):
            far = 7 - k
            step = (far + 1) // 2
            t = lax.rem(me // 4 + 8 + step * (1 - 2 * lax.rem(far, 2)), 8)
            lhs = jnp.concatenate([strips[h, s] for s in range(S)], axis=1)
            out = jnp.dot(lhs, first[t], preferred_element_type=F32)
            for pair in range(2):
                tile = out[:, 128 * pair : 128 * pair + 128]
                for half in range(2):
                    firsts = []
                    seconds = []
                    for gp in (2 * half, 2 * half + 1):
                        even = tile[16 * gp : 16 * gp + 8]
                        odd = tile[16 * gp + 8 : 16 * gp + 16]
                        firsts.append(jnp.where(left, even, pltpu.roll(odd, 64, 1)))
                        seconds.append(jnp.where(left, pltpu.roll(even, 64, 1), odd))
                    lines[h, 4 * t + 2 * pair, half] = jnp.concatenate(firsts, axis=0).astype(BF)
                    lines[h, 4 * t + 2 * pair + 1, half] = jnp.concatenate(seconds, axis=0).astype(BF)
            for i in range(4):
                to = 4 * t + i

                @pl.when(to != me)
                def _():
                    line_copy(h, to).start()

                @pl.when(to == me)
                def _():
                    line_local(h).start()

    def column_transform(h):
        line_local(h).wait()

        @pl.loop(1, B)
        def _(k):
            at = lax.rem(me + k, B)
            remote(
                lines.at[h, at], lrec.at[h, at], li_send.at[h, at], li_recv.at[h, at], (v, at // S, lax.rem(at, S))
            ).wait_recv()

        pieces = []
        for half in range(2):
            wide = lrec[h, :, half].astype(F32)
            for gp in range(2):
                pieces.append(wide[:, 8 * gp : 8 * gp + 8].reshape(256, 128).astype(BF))
        arrived = jnp.concatenate(pieces, axis=1)
        lhs = lax.dot_general(perm[...], arrived, (((1,), (1,)), ((), ())), preferred_element_type=F32).astype(BF)

        @pl.loop(0, 4, unroll=4)
        def _(t):
            lanes = pl.ds(pl.multiple_of(t * 256, 256), 256)
            spec[h, :, lanes] = jnp.dot(lhs, cols[h, :, lanes], preferred_element_type=F32)

    def gather_kernel_x():
        for copy in k2:
            copy.wait_recv()
        mine = pl.ds(4 * v, 4)
        for k in range(1, 4):
            remote(
                krec.at[mine], krec.at[mine], k_send.at[3 + k], k_recv.at[3 + k], (lax.rem(v + 2 * k, V), y, z)
            ).start()
        remote(krec.at[mine], krec.at[mine], k_send.at[8], k_recv.at[8], (sibling, y, z)).start()

    def k2_arrival(k):
        at = pl.ds(4 * lax.rem(v - 2 * k + V, V), 4)
        return remote(
            krec.at[at], krec.at[at], k_send.at[3 + k], k_recv.at[3 + k], (lax.rem(v + 2 * k, V), y, z)
        )

    def gather_kernel_core():
        for k in range(1, 4):
            k2_arrival(k).wait_recv()
            at = pl.ds(4 * lax.rem(v - 2 * k + V, V), 4)
            remote(krec.at[at], krec.at[at], k_send.at[8 + k], k_recv.at[8 + k], (sibling, y, z)).start()

    def k3_arrival(k):
        at = pl.ds(4 * lax.rem(sibling - 2 * k + V, V), 4)
        return remote(krec.at[at], krec.at[at], k_send.at[8 + k], k_recv.at[8 + k], (sibling, y, z))

    def rs_start(h):
        for copy in rs[h][:4]:
            copy.start()

    def rs_sent(h):
        for copy in rs[h]:
            copy.wait_send()

    thicknesses(0, op)
    rs[0][0].start()
    rs[0][1].start()
    thicknesses(1, op)
    rs[1][0].start()
    rs[1][1].start()
    thicknesses(0, up)
    thicknesses(0, dn)
    rs[0][2].start()
    rs[0][3].start()
    for copy in loads:
        copy.start()
    thicknesses(0, y)
    thicknesses(1, up)
    thicknesses(1, dn)
    thicknesses(1, y)
    thicknesses(2, op)
    rs_add(0)
    rs[1][2].start()
    rs[1][3].start()
    rs[2][0].start()
    rs[2][1].start()
    thicknesses(2, up)
    thicknesses(2, dn)
    thicknesses(3, op)
    rs_add(1)
    rs[2][2].start()
    rs[2][3].start()
    rs[3][0].start()
    rs[3][1].start()
    thicknesses(2, y)
    thicknesses(3, up)
    thicknesses(3, dn)
    thicknesses(3, y)
    make_source(0)
    rs_add(2)
    rs[3][2].start()
    rs[3][3].start()
    make_source(1)
    loads[0].wait()
    make_lines(0)
    rs_add(3)
    make_source(2)
    turn_kernel()
    make_lines(1)
    make_source(3)
    make_lines(2)
    gather_kernel_x()
    make_lines(3)
    loads[1].wait()
    loads[5].wait()
    loads[6].wait()
    loads[7].wait()
    column_transform(0)
    gather_kernel_core()
    column_transform(1)
    column_transform(2)
    column_transform(3)
    for k in range(4):
        k3_arrival(k).wait_recv()
    loads[2].wait()
    loads[3].wait()

    def mix(mp, special):
        rows = 16 * mp if special else pl.multiple_of(mp * 16, 16)
        slots = pl.ds(2 * mp, 2)

        def kernel_tile(ref_slice):
            return ref_slice.astype(F32).reshape(16, 128)

        if special:
            row = lax.broadcasted_iota(jnp.int32, (16, 128), 0)
            chosen = row + 8 * me < 8
        for u in range(F // 128):
            lanes = pl.ds(128 * u, 128)
            sins = pl.ds(F + 128 * u, 128)
            vals = []
            for rows_at in (pl.ds(rows, 16), pl.ds(256 + rows, 16)):
                cos = [spec[h, rows_at, lanes] for h in range(H)]
                sin = [spec[h, rows_at, sins] for h in range(H)]
                c0, c1, d0, d1 = cos[0] + cos[2], cos[0] - cos[2], cos[1] + cos[3], cos[1] - cos[3]
                s0, s1, t0, t1 = sin[0] + sin[2], sin[0] - sin[2], sin[1] + sin[3], sin[1] - sin[3]
                vals.append(
                    (
                        (c0 + d0, s0 + t0),
                        (c1 - t1, s1 + d1),
                        (c0 - d0, s0 - t0),
                        (c1 + t1, s1 - d1),
                    )
                )
            for k in range(H):
                (a, c), (b, d) = vals[0][k], vals[1][k]
                plus_r, plus_i = a + d, b - c
                minus_r, minus_i = a - d, b + c
                if special:
                    plus_r = jnp.where(chosen, a, plus_r)
                    plus_i = jnp.where(chosen, -c, plus_i)
                    minus_r = jnp.where(chosen, b, minus_r)
                    minus_i = jnp.where(chosen, d, minus_i)
                at = pl.ds(F * k + 128 * u, 128)
                kr = kernel_tile(kown[0, slots, :, at])
                ki = kernel_tile(kown[1, slots, :, at])
                lr = kernel_tile(krec[slots, 0, :, at])
                li = kernel_tile(krec[slots, 1, :, at])
                mr = kr * plus_r - ki * plus_i
                mi = kr * plus_i + ki * plus_r
                nr = lr * minus_r + li * minus_i
                ni = li * minus_r - lr * minus_i
                x1, x2, x3, x4 = mr + nr, mi + ni, mi - ni, mr - nr
                if special:
                    x1 = jnp.where(chosen, mr, x1)
                    x2 = jnp.where(chosen, mi, x2)
                    x3 = jnp.where(chosen, nr, x3)
                    x4 = jnp.where(chosen, -ni, x4)
                for i, x in enumerate((x1, x2, x3, x4)):
                    prod[i, pl.ds(rows, 16), at] = x.astype(BF)

    mix(0, True)

    @pl.loop(1, 16, unroll=3)
    def _(mp):
        mix(mp, False)

    sums = []
    for i in range(4):
        full = jnp.dot(ones[...], prod[i], preferred_element_type=F32) * SCALE
        sums.append([full[:, F * k : F * k + F] for k in range(H)])
    u1, u2, u3, u4 = sums

    def turned(h, one, other):
        total = one[0]
        for k in range(1, H):
            by = h * k % 4
            term = one[k] if by % 2 == 0 else other[k]
            total = total + term if by < 2 else total - term
        return total

    def negative(values):
        return [-value for value in values]

    sides = []
    for hh in range(2):
        both = []
        for h in (2 * hh, 2 * hh + 1):
            real = [turned(h, u1, negative(u2)), turned(h, negative(u2), negative(u1))]
            imag = [turned(h, u3, u4), turned(h, u4, negative(u3))]
            wide = jnp.concatenate(
                [jnp.concatenate(real, axis=1), jnp.concatenate(imag, axis=1)], axis=0
            ).astype(BF)
            both.append(jnp.dot(wide, cols_t[h], preferred_element_type=F32))
        sides.append(jnp.concatenate(both, axis=0).T.reshape(B, 8, 128))
    back[...] = jnp.concatenate(sides, axis=1).astype(BF)

    def back_copy(to):
        return remote(back.at[to], brec.at[me], ba_send.at[to], ba_recv.at[me], (v, to // S, lax.rem(to, S)))

    @pl.loop(1, B // 2)
    def _(k):
        back_copy(lax.rem(me + k, B)).start()
        back_copy(lax.rem(me + B - k, B)).start()

    back_copy(lax.rem(me + B // 2, B)).start()
    brec[me] = back[me]
    loads[4].wait()

    @pl.loop(1, B)
    def _(k):
        at = lax.rem(me + k, B)
        remote(back.at[at], brec.at[at], ba_send.at[at], ba_recv.at[at], (v, at // S, lax.rem(at, S))).wait_recv()

    even = []
    odd = []
    for dp in range(B // 2):
        b0 = brec[2 * dp].astype(F32)
        b1 = brec[2 * dp + 1].astype(F32)
        even.append(jnp.where(left16, b0, pltpu.roll(b1, 64, 1)).astype(BF))
        odd.append(jnp.where(left16, pltpu.roll(b0, 64, 1), b1).astype(BF))
    lhs = jnp.concatenate([jnp.concatenate(even, axis=1), jnp.concatenate(odd, axis=1)], axis=0)
    for t in range(4):
        lanes = pl.ds(256 * t, 256)
        image = jnp.dot(lhs, last[:, lanes], preferred_element_type=F32) * SCALE
        for half in range(2):
            tile = 2 * t + half
            for hl in range(2):
                for hh in range(2):
                    row = 16 * hl + 8 * hh
                    woven[tile, pl.ds(2 * hh + hl, 8, stride=H), :] = image[row : row + 8, 128 * half : 128 * half + 128]
            scat_ref[:, pl.ds(128 * tile, 128)] = woven[tile]

    for h in range(H):
        rs_sent(h)

        @pl.loop(1, S)
        def _(k):
            strip_copy(h, lax.rem(z + k, S)).wait_send()

        @pl.loop(1, B)
        def _(k):
            line_copy(h, lax.rem(me + k, B)).wait_send()

    for copy in k1[1:] + k2:
        copy.wait_send()

    @pl.when(v > 0)
    def _():
        k1[0].wait_send()

    for k in range(1, 4):
        k2_arrival(k).wait_send()
    for k in range(4):
        k3_arrival(k).wait_send()

    @pl.loop(1, B)
    def _(k):
        back_copy(lax.rem(me + k, B)).wait_send()


def finish_kernel(prim_in, scat_in, prim_out, scat_out):
    prim_out[...] = prim_in[...]
    scat_out[...] = scat_in[...]


def shards(attenuation, material, tilt, kernel_spectra):
    first, cols, cols_t, last, perm, ones = (jnp.asarray(t) for t in tables())
    vmem = pl.BlockSpec(memory_space=pltpu.VMEM)
    hbm = pl.BlockSpec(memory_space=pl.ANY)
    dma = pltpu.SemaphoreType.DMA
    shapes = (jax.ShapeDtypeStruct((H * PART, 128), F32), jax.ShapeDtypeStruct((Q, N), F32))
    results = pl.pallas_call(
        main_kernel,
        out_shape=shapes,
        in_specs=[pl.BlockSpec(memory_space=pltpu.SMEM), hbm, hbm, hbm, hbm, hbm, hbm, hbm, hbm, hbm],
        out_specs=(vmem, vmem),
        scratch_shapes=[
            pltpu.VMEM((4, N, 128), BF),
            pltpu.VMEM((4, N + 2 * EDGE, 128), F32),
            pltpu.VMEM((4, N + 2 * EDGE, 128), jnp.int32),
            pltpu.VMEM((H, D, G, PART, 128), BF),
            pltpu.VMEM((8, N, 256), BF),
            pltpu.VMEM((H, N // H, 2 * F), BF),
            pltpu.VMEM((H, 2 * F, N // H), BF),
            pltpu.VMEM((PAD, N), BF),
            pltpu.VMEM((512, 512), BF),
            pltpu.VMEM((Q, Q * G), BF),
            pltpu.VMEM((2, Q, G, PAD), BF),
            pltpu.VMEM((Q, 2, G, PAD), BF),
            pltpu.VMEM((4, 2, G, PAD), BF),
            pltpu.VMEM((H, 2, 4, PART, 128), BF),
            pltpu.VMEM((H, 2, 4, PART, 128), BF),
            pltpu.VMEM((H, G, PART, 128), BF),
            pltpu.VMEM((H, G, PART, 128), BF),
            pltpu.VMEM((H, S, 64, 128), BF),
            pltpu.VMEM((H, S, 64, 128), BF),
            pltpu.VMEM((H, B, 2, 16, 128), BF),
            pltpu.VMEM((H, B, 2, 16, 128), BF),
            pltpu.VMEM((H, 512, 2 * F), F32),
            pltpu.VMEM((4, Q * G, PAD), BF),
            pltpu.VMEM((B, 16, 128), BF),
            pltpu.VMEM((B, 16, 128), BF),
            pltpu.VMEM((8, Q, 128), F32),
            dma((4,)),
            dma((8,)),
            dma((H, 6)),
            dma((H, 6)),
            dma((H, S)),
            dma((H, S)),
            dma((H, B)),
            dma((H, B)),
            dma((B,)),
            dma((B,)),
            dma((16,)),
            dma((16,)),
        ],
        compiler_params=pltpu.CompilerParams(
            collective_id=0, has_side_effects=True, vmem_limit_bytes=60 * 2**20
        ),
        name="scatter",
    )(tilt, attenuation, material, kernel_spectra, first, cols, cols_t, last, perm, ones)
    return pl.pallas_call(
        finish_kernel,
        out_shape=shapes,
        in_specs=[vmem, vmem],
        out_specs=(vmem, vmem),
        name="finish",
    )(*results)


def solution(mesh):
    return jax.shard_map(
        shards,
        mesh=mesh,
        in_specs=(
            P(("view", "depth"), None, "stripe"),
            P(("view", "depth"), None, "stripe"),
            P("view"),
            P(None, ("depth", "stripe"), None, None),
        ),
        out_specs=(P(("view", "depth"), "stripe"), P(("view", "depth", "stripe"), None)),
        check_vma=False,
    )
```
